128 devices in a mesh: row: 8 (over z_hi, x), col: 16 (over y, z_lo, core).
Axes of the slice: x: 4, y: 4, z: 4 (z_hi: 2, z_lo: 2; z = z_hi * 2 + z_lo), core: 2. Of those that a mesh axis runs over, the one named last changes fastest.
Arguments:
- occupancy: int32 [128, 128], replicated, may hold values from 0 to 1, as said below
- stored: bfloat16 [8, 16, 8, 256, 256], P('row', 'col'), as said below
Outputs:
- window: float32 [4096, 32768], P('row', 'col')
The draws below stay inside these ranges and needn't reach their ends.
Inputs may be any that keep to these rules, and one draw needn't show every extreme that they name: occupancy[i, j] is 0 where i > j. Each tile holds at most 8 blocks with occupancy 1, and tile (0, 15) holds exactly 8. Slots past a tile's number of occupied blocks are zero; stored blocks on the diagonal are symmetric.
All inputs are finite; a program needn't handle non-finite values.
Results may differ from the reference program's by a relative error of at most 0.0003.
Values may be sent and summed in bfloat16 or wider, within the bound.
No kernel may reach another device: no remote copies, remote signals or barrier semaphores. Data moves between devices by JAX's collectives and lax.ppermute only.
A program may use at most 768 MiB of HBM per device.

```python
import jax
import jax.numpy as jnp
from jax import lax

BS = 256
CB = 8
SLOTS = 8
SR = 2
NB = 128
N_ROW = 8
N_COL = 16


def occupancy_tiles(key):
    row_blocks = 2 * CB
    positions = row_blocks * CB
    panel_index = jnp.arange(N_ROW, dtype=jnp.int32)[:, None, None, None]
    column_index = jnp.arange(N_COL, dtype=jnp.int32)[None, :, None, None]
    local_row = jnp.arange(row_blocks, dtype=jnp.int32)[None, None, :, None]
    local_col = jnp.arange(CB, dtype=jnp.int32)[None, None, None, :]
    global_row = (local_row // CB * N_ROW + panel_index) * CB + local_row % CB
    global_col = column_index * CB + local_col
    usable = (global_row <= global_col).reshape(N_ROW, N_COL, positions)
    first_key, second_key = jax.random.split(key)
    wanted = jax.random.randint(first_key, (N_ROW, N_COL), SLOTS - SLOTS // 4, SLOTS + 1)
    wanted = wanted.at[0, N_COL - 1].set(SLOTS)
    scores = jax.random.randint(second_key, (N_ROW, N_COL, positions), 0, 1 << 20) * positions + jnp.arange(positions, dtype=jnp.int32)
    scores = jnp.where(usable, scores, -1)
    ranking = jnp.sum((scores[:, :, None, :] > scores[:, :, :, None]).astype(jnp.int32), axis=3)
    return (usable & (ranking < wanted[:, :, None])).astype(jnp.int32)


def draw_occupancy(key, part):
    tiles = occupancy_tiles(jax.random.fold_in(key, 11))
    block_row = jnp.arange(NB, dtype=jnp.int32)[:, None]
    block_col = jnp.arange(NB, dtype=jnp.int32)[None, :]
    panel_index = block_row // CB % N_ROW
    local_row = block_row // CB // N_ROW * CB + block_row % CB
    return tiles[panel_index, block_col // CB, local_row * CB + block_col % CB]


def draw_stored(key, part):
    tiles = occupancy_tiles(jax.random.fold_in(key, 11))
    running = jnp.cumsum(tiles, axis=2)
    wanted = jnp.arange(SLOTS, dtype=jnp.int32)
    position = jnp.sum((running[:, :, None, :] <= wanted[None, None, :, None]).astype(jnp.int32), axis=3)
    present = wanted[None, None, :] < running[:, :, -1:]
    position = jnp.minimum(position, 2 * CB * CB - 1)
    local_row = position // CB
    local_col = position % CB
    panel_index = jnp.arange(N_ROW, dtype=jnp.int32)[:, None, None]
    column_index = jnp.arange(N_COL, dtype=jnp.int32)[None, :, None]
    global_row = (local_row // CB * N_ROW + panel_index) * CB + local_row % CB
    global_col = column_index * CB + local_col
    diagonal = global_row == global_col
    shape = (N_ROW, N_COL, SLOTS, BS, BS)
    values = jax.random.normal(jax.random.fold_in(key, 23), shape, jnp.float32)
    values = values * 0.25
    symmetric = (values + jnp.swapaxes(values, 3, 4)) * 0.70710678
    values = jnp.where(diagonal[:, :, :, None, None], symmetric, values) * present[:, :, :, None, None].astype(jnp.float32)
    return values.astype(jnp.bfloat16)


def setup_inputs(seed: int = 0) -> dict:
    seeds = jax.random.split(jax.random.key(seed), 3)
    occupancy = draw_occupancy(jax.random.fold_in(seeds[2], 71), 0)
    stored = draw_stored(jax.random.fold_in(seeds[2], 71), 0)
    return dict(occupancy=occupancy, stored=stored)


def panel_blocks(row_panel):
    leading = row_panel * CB + jnp.arange(CB, dtype=jnp.int32)
    return jnp.concatenate([leading, leading + N_ROW * CB])


def tile_occupancy(pattern, row_panel, column):
    picked = jnp.take(pattern, panel_blocks(row_panel), axis=0)
    return lax.dynamic_slice_in_dim(picked, (column * CB).astype(jnp.int32), CB, 1)


def unpack(packed, occupied):
    flat_mask = occupied.reshape(-1)
    position = jnp.clip(jnp.cumsum(flat_mask) - 1, 0, packed.shape[0] - 1).astype(jnp.int32)
    pieces = jnp.take(packed, position, axis=0) * flat_mask[:, None, None].astype(packed.dtype)
    row_blocks, col_blocks = occupied.shape
    edge = packed.shape[1]
    return pieces.reshape(row_blocks, col_blocks, edge, edge).transpose(0, 2, 1, 3).reshape(row_blocks * edge, col_blocks * edge)


def assemble(upper_part, mirror, partner, col_half, row_panel, column):
    breadth = mirror.shape[1]
    from_mirror = lax.dynamic_slice_in_dim(mirror, (col_half * breadth).astype(jnp.int32), breadth, 0).T
    from_partner = lax.dynamic_slice_in_dim(partner, (col_half * breadth).astype(jnp.int32), breadth, 0).T
    lower_part = jnp.where(col_half == 0, jnp.concatenate([from_mirror, from_partner], 0), jnp.concatenate([from_partner, from_mirror], 0))
    block_rows = panel_blocks(row_panel)
    block_cols = column * CB + jnp.arange(CB, dtype=jnp.int32)
    strictly = (block_rows[:, None] > block_cols[None, :]).astype(lower_part.dtype)
    edge = breadth // CB
    count_rows = block_rows.shape[0]
    lower_part = (lower_part.reshape(count_rows, edge, CB, edge) * strictly[:, None, :, None]).reshape(count_rows * edge, breadth)
    return upper_part + lower_part


def dense_tile(pattern, stored, row_panel, column):
    source_row = column % N_ROW
    col_half = column // N_ROW
    here_col = row_panel + N_ROW * col_half
    there_col = row_panel + N_ROW * (1 - col_half)
    upper_part = unpack(stored[row_panel, column], tile_occupancy(pattern, row_panel, column))
    mirror = unpack(stored[source_row, here_col], tile_occupancy(pattern, source_row, here_col))
    partner = unpack(stored[source_row, there_col], tile_occupancy(pattern, source_row, there_col))
    return assemble(upper_part, mirror, partner, col_half, row_panel, column)


def reference(occupancy, stored):
    slab_rows = SR * BS

    def per_device(device):
        row_panel = device // N_COL
        column = device % N_COL
        result = jnp.zeros((slab_rows, CB * BS), jnp.float32)
        for section in range(2):
            middle = (row_panel + column + section) % N_ROW
            first_half = dense_tile(occupancy, stored, row_panel, middle)[:slab_rows]
            second_half = dense_tile(occupancy, stored, row_panel, middle + N_ROW)[:slab_rows]
            factor_left = jnp.concatenate([first_half, second_half], 1)
            factor_right = dense_tile(occupancy, stored, middle, column)
            result = result + jnp.dot(factor_left, factor_right, preferred_element_type=jnp.float32)
        return result

    gathered = lax.map(per_device, jnp.arange(N_ROW * N_COL, dtype=jnp.int32))
    return gathered.reshape(N_ROW, N_COL, slab_rows, CB * BS).transpose(0, 2, 1, 3).reshape(N_ROW * slab_rows, N_COL * CB * BS)
```

```python
import functools

import jax
import jax.numpy as jnp
import numpy as np
from jax import lax
from jax.experimental import pallas as pl
from jax.experimental.pallas import tpu as pltpu
from jax.sharding import PartitionSpec as P

BS = 256
CB = 8
SLOTS = 8
SR = 2
NB = 128
NR = 8
NC = 16
GROUPS = "ABCDEF"


def routes():
    plan = []
    for s in range(2):
        g = {n: [] for n in GROUPS}
        for a in range(NR):
            for b in range(NC):
                k = (a + b + s) % NR
                here = a * NC + b
                low = b < NR
                up = a <= k
                if not low or k <= b:
                    g["A"].append((k * NC + b, here))
                else:
                    g["B"].append((b * NC + k, here))
                if low:
                    g["C"].append((b * NC + k + NR, here))
                elif k + NR > b:
                    g["B"].append(((b - NR) * NC + k + NR, here))
                g["D" if low else "E"].append((a * NC + k + NR, here))
                name = {(False, True): "C", (False, False): "D", (True, True): "E", (True, False): "F"}[(low, up)]
                g[name].append((a * NC + k if up else k * NC + a, here))
        plan.append(g)
    return plan


def slot_table(occupancy):
    i = np.arange(NB)
    before_col = (i[:, None] // CB == i[None, :] // CB) & (i[:, None] < i[None, :])
    panel = i[:, None] // CB == i[None, :] // CB
    before_row = (i[:, None] // CB % NR == i[None, :] // CB % NR) & (i[None, :] < i[:, None])
    occ = occupancy.astype(jnp.float32)
    dot = functools.partial(jnp.dot, precision=lax.Precision.HIGHEST)
    rank = dot(occ, jnp.asarray(before_col, jnp.float32)) + dot(
        jnp.asarray(before_row, jnp.float32), dot(occ, jnp.asarray(panel, jnp.float32))
    )
    return jnp.where(occupancy == 1, rank.astype(jnp.int32), -1)


def product_kernel(table, *refs):
    bufs = refs[:12]
    out, tiles, left, sems = refs[12:]
    a = lax.axis_index("row")
    b = lax.axis_index("col")
    low = b < NR
    n = {g: i for i, g in enumerate(GROUPS)}

    def fetch(cond, s, name, kind):
        @pl.when(cond)
        def _():
            pltpu.make_async_copy(bufs[6 * s + n[name]], tiles.at[4 * s + kind], sems.at[4 * s + kind]).start()

    for s in range(2):
        k = lax.rem(a + b + s, NR)
        up = a <= k
        high = jnp.logical_not(low)
        straight = jnp.logical_or(high, k <= b)
        fetch(straight, s, "A", 0)
        fetch(jnp.logical_not(straight), s, "B", 0)
        fetch(low, s, "C", 1)
        fetch(jnp.logical_and(high, k + NR <= b), s, "A", 1)
        fetch(jnp.logical_and(high, k + NR > b), s, "B", 1)
        fetch(jnp.logical_and(low, up), s, "E", 2)
        fetch(jnp.logical_and(low, jnp.logical_not(up)), s, "F", 2)
        fetch(jnp.logical_and(high, up), s, "C", 2)
        fetch(jnp.logical_and(high, jnp.logical_not(up)), s, "D", 2)
        fetch(low, s, "D", 3)
        fetch(high, s, "E", 3)
    out[...] = jnp.zeros_like(out)
    for t in range(8):
        pltpu.make_async_copy(bufs[0], tiles.at[t], sems.at[t]).wait()

    def step(t, carry):
        s = t // 16
        kk = lax.rem(t, 16)
        half = kk // CB
        k = lax.rem(a + b + s, NR)
        inner = (half * NR + k) * CB + lax.rem(kk, CB)

        def one_row(i, carry):
            row = a * CB + i
            slot = table[jnp.minimum(row, inner), jnp.maximum(row, inner)]

            @pl.when(slot >= 0)
            def _():
                lt = tiles.at[4 * s + 2 + half, slot]

                @pl.when(row <= inner)
                def _():
                    left[...] = lt[...]

                @pl.when(row > inner)
                def _():
                    left[...] = lt[...].T

                def one_col(j, carry):
                    col = b * CB + j
                    rslot = table[jnp.minimum(inner, col), jnp.maximum(inner, col)]

                    @pl.when(rslot >= 0)
                    def _():
                        where = (
                            pl.ds(pl.multiple_of(i * BS, BS), BS),
                            pl.ds(pl.multiple_of(j * BS, BS), BS),
                        )
                        rt = tiles.at[4 * s + half, rslot]

                        @pl.when(inner <= col)
                        def _():
                            out[where] += jnp.dot(left[...], rt[...], preferred_element_type=jnp.float32)

                        @pl.when(inner > col)
                        def _():
                            out[where] += lax.dot_general(
                                left[...], rt[...], (((1,), (1,)), ((), ())), preferred_element_type=jnp.float32
                            )

                    return carry

                lax.fori_loop(0, CB, one_col, 0)

            return carry

        return lax.fori_loop(0, SR, one_row, carry)

    lax.fori_loop(0, 32, step, 0)


def local(occupancy, stored):
    own = stored.reshape(SLOTS, BS, BS)
    table = slot_table(occupancy)
    bufs = []
    for g in routes():
        for name in GROUPS:
            bufs.append(lax.ppermute(own, ("row", "col"), g[name]))
    return pl.pallas_call(
        product_kernel,
        out_shape=jax.ShapeDtypeStruct((SR * BS, CB * BS), jnp.float32),
        in_specs=[pl.BlockSpec(memory_space=pltpu.SMEM)] + [pl.BlockSpec(memory_space=pl.ANY)] * 12,
        out_specs=pl.BlockSpec(memory_space=pltpu.VMEM),
        scratch_shapes=[
            pltpu.VMEM((8, SLOTS, BS, BS), jnp.bfloat16),
            pltpu.VMEM((BS, BS), jnp.bfloat16),
            pltpu.SemaphoreType.DMA((8,)),
        ],
        compiler_params=pltpu.CompilerParams(vmem_limit_bytes=32 * 1024 * 1024),
        cost_estimate=pl.CostEstimate(flops=10**9, bytes_accessed=12 * 2**20, transcendentals=0),
        name="products",
    )(table, *bufs)


def solution(mesh):
    placed = (P(), P("row", "col", None, None, None))
    return jax.shard_map(
        local, mesh=mesh, in_specs=placed, out_specs=P("row", "col"), check_vma=False
    )
```

```python
import functools

import jax
import jax.numpy as jnp
import numpy as np
from jax import lax
from jax.experimental import pallas as pl
from jax.experimental.pallas import tpu as pltpu
from jax.sharding import PartitionSpec as P

BS = 256
CB = 8
SLOTS = 8
SR = 2
NB = 128
NR = 8
NC = 16
ND = NR * NC
MIB = 1024 * 1024
FETCH = 640

FIRST = [
    [
        (1, 9, 1), (3, 48, 3), (4, 52, 4), (5, 4, 5), (6, 96, 6), (7, 113, 7), (10, 32, 10), (11, 75, 11),
        (13, 5, 13), (14, 104, 14), (15, 7, 15), (17, 39, 17), (18, 46, 18), (19, 18, 19), (20, 68, 20), (21, 91, 21),
        (22, 29, 22), (23, 21, 23), (24, 23, 24), (25, 24, 25), (26, 17, 26), (27, 26, 27), (28, 92, 28), (29, 28, 29),
        (30, 65, 30), (31, 22, 31), (35, 54, 35), (36, 41, 36), (37, 35, 37), (38, 100, 38), (39, 37, 39), (40, 45, 40),
        (41, 114, 41), (42, 122, 42), (43, 107, 43), (44, 33, 44), (45, 77, 45), (46, 78, 46), (47, 44, 47), (51, 63, 51),
        (52, 71, 52), (53, 86, 53), (54, 58, 54), (56, 67, 56), (57, 83, 57), (58, 10, 58), (59, 119, 59), (60, 57, 60),
        (61, 109, 61), (62, 50, 62), (63, 60, 63), (68, 64, 68), (69, 87, 69), (70, 20, 70), (71, 124, 71), (72, 76, 72),
        (73, 69, 73), (75, 70, 75), (76, 79, 76), (77, 72, 77), (78, 1, 78), (79, 36, 79), (85, 117, 85), (86, 103, 86),
        (87, 82, 87), (88, 53, 88), (89, 84, 89), (90, 93, 90), (91, 27, 91), (92, 101, 92), (93, 125, 93), (94, 80, 94),
        (95, 90, 95), (102, 118, 102), (103, 97, 103), (104, 88, 104), (105, 98, 105), (106, 99, 106), (107, 43, 107), (108, 47, 108),
        (109, 111, 109), (110, 14, 110), (119, 123, 119), (121, 105, 121), (122, 55, 122), (124, 127, 124), (127, 112, 127),
    ],
    [
        (1, 97, 1), (2, 16, 2), (3, 2, 3), (4, 48, 4), (5, 82, 5), (6, 5, 6), (7, 6, 7), (9, 1, 9),
        (10, 9, 10), (11, 56, 11), (14, 30, 14), (17, 113, 17), (18, 38, 18), (19, 54, 19), (20, 27, 20), (21, 69, 21),
        (22, 21, 22), (23, 121, 23), (24, 8, 24), (25, 20, 25), (26, 24, 26), (28, 19, 28), (29, 49, 29), (30, 73, 30),
        (31, 81, 31), (34, 51, 34), (35, 18, 35), (36, 100, 36), (37, 84, 37), (38, 99, 38), (39, 66, 39), (40, 37, 40),
        (41, 25, 41), (42, 39, 42), (43, 10, 43), (45, 43, 45), (46, 44, 46), (47, 108, 47), (51, 115, 51), (52, 3, 52),
        (53, 57, 53), (54, 50, 54), (55, 52, 55), (56, 40, 56), (57, 53, 57), (58, 62, 58), (59, 55, 59), (60, 28, 60),
        (61, 58, 61), (62, 35, 62), (69, 101, 69), (70, 102, 70), (71, 67, 71), (73, 41, 73), (74, 26, 74), (75, 116, 75),
        (76, 64, 76), (77, 4, 77), (78, 65, 78), (79, 75, 79), (85, 88, 85), (86, 80, 86), (87, 90, 87), (88, 91, 88),
        (89, 92, 89), (90, 72, 90), (91, 94, 91), (92, 86, 92), (93, 13, 93), (94, 78, 94), (95, 45, 95), (102, 22, 102),
        (103, 127, 103), (104, 98, 104), (105, 89, 105), (106, 74, 106), (107, 109, 107), (110, 126, 110), (111, 105, 111), (119, 7, 119),
        (121, 114, 121), (122, 123, 122), (123, 59, 123), (124, 117, 124), (126, 14, 126),
    ],
    [
        (0, 4, 0), (1, 22, 1), (2, 46, 2), (3, 10, 3), (4, 64, 4), (5, 37, 5), (6, 14, 6), (7, 23, 7),
        (8, 7, 8), (9, 105, 9), (10, 90, 10), (11, 2, 11), (12, 56, 12), (13, 45, 13), (15, 112, 15), (17, 16, 17),
        (18, 114, 18), (19, 26, 19), (20, 19, 20), (21, 20, 21), (22, 54, 22), (23, 97, 23), (24, 31, 24), (25, 121, 25),
        (26, 9, 26), (27, 18, 27), (28, 27, 28), (29, 73, 29), (30, 28, 30), (31, 89, 31), (34, 32, 34), (35, 62, 35),
        (36, 33, 36), (38, 36, 38), (39, 42, 39), (40, 98, 40), (41, 38, 41), (42, 47, 42), (43, 40, 43), (44, 41, 44),
        (46, 35, 46), (51, 3, 51), (52, 116, 52), (53, 49, 53), (54, 70, 54), (55, 51, 55), (56, 52, 56), (57, 61, 57),
        (58, 127, 58), (60, 124, 60), (62, 58, 62), (63, 79, 63), (68, 71, 68), (69, 65, 69), (70, 74, 70), (71, 117, 71),
        (72, 8, 72), (73, 77, 73), (74, 78, 74), (75, 11, 75), (76, 1, 76), (77, 12, 77), (78, 44, 78), (79, 66, 79),
        (85, 80, 85), (86, 21, 86), (87, 81, 87), (88, 83, 88), (89, 57, 89), (91, 101, 91), (93, 88, 93), (94, 24, 94),
        (95, 94, 95), (102, 111, 102), (103, 104, 103), (104, 43, 104), (105, 106, 105), (106, 108, 106), (107, 86, 107), (108, 110, 108),
        (109, 29, 109), (110, 96, 110), (111, 30, 111), (120, 113, 120), (121, 39, 121), (122, 115, 122), (123, 75, 123), (124, 60, 124),
        (125, 118, 125), (127, 122, 127),
    ],
    [
        (1, 16, 1), (2, 10, 2), (3, 67, 3), (4, 11, 4), (5, 12, 5), (6, 38, 6), (7, 15, 7), (8, 57, 8),
        (9, 24, 9), (10, 2, 10), (11, 48, 11), (12, 76, 12), (13, 88, 13), (14, 6, 14), (15, 120, 15), (17, 1, 17),
        (18, 25, 18), (19, 83, 19), (20, 33, 20), (21, 28, 21), (22, 81, 22), (23, 22, 23), (27, 107, 27), (28, 41, 28),
        (29, 19, 29), (30, 20, 30), (31, 47, 31), (34, 39, 34), (35, 32, 35), (36, 70, 36), (37, 42, 37), (38, 43, 38),
        (39, 123, 39), (41, 46, 41), (43, 26, 43), (44, 92, 44), (45, 34, 45), (46, 62, 46), (47, 36, 47), (52, 56, 52),
        (53, 50, 53), (54, 101, 54), (55, 116, 55), (56, 53, 56), (57, 9, 57), (58, 54, 58), (60, 3, 60), (61, 49, 61),
        (62, 94, 62), (68, 72, 68), (69, 117, 69), (70, 66, 70), (71, 87, 71), (72, 75, 72), (73, 84, 73), (74, 69, 74),
        (75, 79, 75), (76, 124, 76), (77, 65, 77), (78, 74, 78), (79, 60, 79), (85, 5, 85), (86, 89, 86), (87, 37, 87),
        (89, 73, 89), (90, 85, 90), (92, 95, 92), (93, 80, 93), (94, 29, 94), (95, 82, 95), (102, 103, 102), (103, 118, 103),
        (104, 105, 104), (105, 99, 105), (106, 58, 106), (107, 100, 107), (108, 109, 108), (109, 102, 109), (110, 111, 110), (111, 96, 111),
        (119, 112, 119), (120, 7, 120), (121, 122, 121), (122, 90, 122), (123, 115, 123), (125, 45, 125), (126, 119, 126), (127, 63, 127),
    ],
]
SECOND = [
    [
        (0, 112, 0), (1, 20, 78), (3, 11, 60), (4, 8, 0), (7, 0, 8), (9, 40, 10), (10, 2, 43), (12, 60, 12),
        (14, 13, 14), (15, 31, 15), (16, 1, 2), (18, 17, 18), (19, 33, 19), (20, 110, 70), (21, 5, 86), (22, 6, 102),
        (23, 22, 24), (24, 23, 25), (25, 24, 18), (26, 18, 43), (27, 26, 28), (28, 29, 30), (29, 28, 22), (30, 46, 30),
        (31, 30, 24), (32, 16, 10), (33, 49, 20), (35, 50, 37), (37, 117, 87), (38, 70, 38), (39, 36, 39), (40, 32, 43),
        (42, 43, 37), (43, 108, 38), (44, 66, 47), (45, 37, 95), (46, 47, 41), (47, 63, 47), (48, 12, 4), (50, 93, 53),
        (51, 114, 34), (52, 57, 52), (53, 101, 53), (54, 35, 54), (56, 79, 52), (57, 53, 89), (58, 59, 62), (59, 55, 123),
        (60, 48, 60), (61, 62, 57), (62, 41, 35), (63, 51, 63), (64, 67, 4), (65, 81, 30), (66, 82, 39), (68, 69, 20),
        (69, 72, 69), (70, 86, 54), (71, 52, 71), (72, 58, 90), (73, 27, 29), (74, 73, 78), (75, 56, 72), (76, 64, 12),
        (77, 109, 77), (78, 77, 74), (79, 75, 63), (80, 89, 94), (81, 125, 87), (82, 21, 95), (83, 61, 19), (84, 83, 89),
        (85, 42, 90), (86, 85, 53), (87, 4, 69), (88, 95, 85), (89, 91, 89), (90, 106, 10), (91, 90, 88), (92, 76, 28),
        (93, 92, 90), (94, 78, 62), (95, 111, 95), (96, 97, 111), (97, 96, 103), (99, 44, 38), (100, 84, 36), (101, 100, 54),
        (102, 104, 102), (103, 102, 86), (104, 88, 14), (105, 38, 105), (107, 25, 27), (109, 19, 61), (110, 103, 110), (112, 7, 127),
        (113, 120, 7), (114, 98, 41), (115, 116, 123), (116, 115, 55), (117, 71, 124), (118, 87, 125), (119, 118, 126), (120, 121, 120),
        (121, 113, 25), (122, 74, 122), (123, 122, 39), (125, 126, 125), (127, 99, 58),
    ],
    [
        (1, 0, 9), (3, 52, 3), (4, 7, 0), (7, 112, 8), (9, 8, 1), (10, 60, 3), (11, 10, 11), (12, 48, 12),
        (13, 95, 93), (15, 14, 7), (16, 98, 2), (17, 16, 26), (18, 2, 35), (19, 18, 20), (20, 84, 21), (21, 107, 22),
        (22, 23, 1), (23, 30, 23), (24, 5, 94), (25, 31, 25), (26, 25, 19), (27, 43, 91), (28, 27, 60), (29, 13, 94),
        (30, 22, 111), (31, 97, 24), (32, 33, 35), (33, 34, 44), (34, 47, 34), (37, 21, 87), (38, 39, 18), (39, 40, 34),
        (40, 24, 40), (41, 42, 44), (42, 92, 37), (43, 38, 104), (44, 36, 78), (45, 29, 125), (46, 45, 2), (47, 28, 108),
        (48, 32, 11), (49, 57, 29), (50, 19, 53), (51, 124, 55), (52, 49, 52), (54, 55, 35), (55, 3, 59), (56, 61, 56),
        (57, 41, 57), (58, 59, 54), (59, 11, 59), (60, 44, 124), (62, 63, 58), (64, 71, 76), (65, 64, 69), (66, 67, 79),
        (67, 75, 71), (69, 53, 21), (70, 77, 36), (71, 4, 68), (72, 73, 77), (73, 89, 30), (74, 70, 106), (75, 74, 79),
        (76, 72, 12), (77, 76, 73), (78, 66, 46), (79, 78, 75), (80, 81, 86), (81, 65, 22), (82, 91, 5), (83, 99, 57),
        (84, 69, 37), (87, 20, 69), (88, 87, 93), (89, 105, 31), (90, 126, 87), (91, 83, 21), (92, 108, 44), (94, 93, 91),
        (95, 94, 92), (96, 80, 6), (97, 113, 1), (98, 82, 40), (99, 50, 38), (100, 54, 38), (101, 109, 54), (102, 103, 109),
        (103, 118, 86), (104, 106, 104), (105, 121, 9), (108, 101, 108), (109, 35, 61), (110, 86, 108), (111, 110, 109), (112, 96, 15),
        (114, 1, 18), (115, 114, 122), (116, 100, 75), (117, 116, 124), (118, 6, 103), (119, 123, 59), (120, 104, 120), (121, 122, 23),
        (122, 119, 127), (124, 125, 71), (125, 117, 93), (126, 127, 126), (127, 115, 58),
    ],
    [
        (1, 4, 76), (2, 1, 10), (3, 19, 52), (4, 20, 77), (5, 72, 13), (6, 5, 14), (7, 23, 120), (9, 25, 57),
        (10, 11, 3), (12, 13, 5), (13, 12, 13), (14, 30, 126), (16, 32, 2), (17, 31, 17), (18, 17, 27), (19, 18, 28),
        (20, 86, 70), (21, 49, 21), (22, 38, 22), (23, 113, 24), (24, 21, 94), (25, 16, 25), (26, 62, 19), (27, 26, 20),
        (28, 27, 21), (29, 106, 22), (30, 6, 111), (31, 29, 31), (32, 99, 35), (34, 35, 45), (35, 34, 37), (36, 52, 79),
        (37, 103, 87), (38, 39, 41), (39, 55, 39), (40, 33, 43), (41, 42, 36), (43, 59, 107), (44, 110, 78), (46, 43, 46),
        (47, 90, 47), (48, 61, 3), (49, 65, 29), (50, 51, 62), (51, 2, 34), (52, 67, 55), (53, 37, 88), (54, 53, 19),
        (56, 60, 56), (57, 58, 53), (58, 54, 106), (59, 56, 59), (60, 44, 79), (61, 57, 61), (62, 50, 46), (63, 15, 127),
        (64, 116, 76), (65, 94, 69), (66, 114, 39), (67, 83, 56), (68, 76, 20), (69, 100, 74), (70, 69, 36), (71, 70, 52),
        (72, 68, 72), (73, 77, 29), (74, 73, 70), (75, 71, 123), (76, 3, 12), (77, 125, 77), (78, 74, 46), (79, 95, 79),
        (82, 64, 5), (83, 82, 88), (85, 84, 90), (86, 87, 92), (87, 118, 87), (88, 80, 13), (89, 88, 86), (90, 24, 10),
        (95, 28, 92), (96, 98, 6), (97, 81, 23), (98, 97, 104), (99, 66, 38), (100, 101, 107), (101, 85, 91), (102, 36, 70),
        (103, 22, 103), (104, 96, 14), (105, 89, 121), (106, 107, 106), (107, 123, 43), (109, 93, 61), (110, 104, 110), (111, 14, 111),
        (113, 112, 120), (115, 48, 51), (118, 117, 125), (119, 115, 59), (121, 9, 25), (122, 40, 42), (124, 108, 60), (127, 120, 127),
    ],
    [
        (1, 0, 1), (2, 3, 11), (3, 19, 60), (4, 53, 5), (5, 4, 13), (6, 22, 6), (7, 6, 15), (8, 15, 8),
        (9, 122, 26), (10, 9, 2), (11, 27, 75), (12, 28, 77), (13, 5, 93), (14, 13, 6), (16, 37, 2), (17, 24, 17),
        (18, 16, 18), (19, 49, 28), (20, 1, 25), (21, 20, 22), (22, 21, 31), (23, 39, 23), (24, 25, 26), (26, 84, 74),
        (27, 77, 20), (28, 33, 28), (30, 80, 14), (32, 115, 35), (33, 18, 36), (34, 50, 45), (36, 82, 47), (37, 38, 40),
        (38, 35, 38), (39, 23, 17), (40, 41, 43), (41, 57, 73), (42, 10, 42), (43, 42, 45), (44, 45, 47), (45, 46, 40),
        (46, 47, 18), (47, 97, 31), (48, 32, 3), (49, 61, 29), (50, 51, 54), (51, 55, 51), (52, 71, 55), (55, 59, 55),
        (56, 40, 11), (57, 120, 8), (58, 43, 62), (59, 63, 59), (60, 52, 63), (62, 58, 46), (64, 76, 4), (65, 64, 77),
        (66, 65, 70), (67, 66, 71), (68, 116, 68), (69, 68, 73), (70, 78, 36), (71, 36, 71), (73, 69, 89), (74, 109, 70),
        (75, 67, 72), (77, 93, 45), (78, 94, 78), (79, 12, 76), (80, 88, 94), (81, 99, 22), (82, 83, 5), (83, 17, 19),
        (84, 85, 37), (85, 87, 85), (86, 70, 107), (87, 95, 69), (88, 72, 88), (89, 110, 86), (90, 89, 95), (91, 86, 91),
        (92, 26, 44), (94, 81, 95), (95, 29, 95), (96, 106, 6), (97, 30, 1), (99, 100, 106), (101, 117, 92), (102, 118, 109),
        (103, 111, 86), (104, 105, 103), (105, 54, 105), (106, 107, 105), (107, 91, 27), (108, 74, 47), (109, 108, 107), (110, 44, 108),
        (111, 127, 111), (113, 96, 7), (114, 98, 18), (115, 56, 51), (116, 123, 55), (117, 73, 69), (118, 103, 125), (119, 48, 59),
        (120, 104, 15), (121, 113, 23), (122, 114, 42), (124, 125, 124), (127, 126, 103),
    ],
    [
        (0, 15, 0), (1, 16, 9), (3, 78, 52), (4, 68, 4), (5, 90, 5), (7, 121, 7), (8, 52, 72), (9, 8, 9),
        (10, 26, 58), (11, 75, 4), (12, 4, 12), (13, 64, 13), (14, 6, 110), (15, 14, 15), (16, 82, 2), (17, 1, 26),
        (18, 33, 27), (19, 20, 29), (20, 21, 30), (21, 29, 23), (22, 31, 1), (24, 106, 26), (25, 9, 41), (26, 42, 74),
        (28, 19, 21), (29, 13, 109), (30, 62, 30), (31, 30, 31), (32, 40, 35), (33, 34, 36), (35, 36, 46), (36, 37, 47),
        (37, 44, 39), (38, 105, 6), (39, 23, 121), (41, 57, 28), (42, 45, 39), (44, 28, 78), (45, 61, 13), (46, 38, 2),
        (47, 2, 42), (48, 53, 3), (49, 50, 61), (50, 35, 53), (51, 60, 55), (52, 48, 52), (53, 54, 57), (54, 55, 58),
        (55, 39, 122), (56, 11, 12), (57, 56, 60), (58, 27, 61), (60, 49, 60), (62, 63, 35), (63, 59, 63), (64, 3, 4),
        (65, 66, 78), (66, 115, 39), (67, 83, 3), (68, 84, 20), (69, 65, 21), (70, 71, 75), (71, 74, 71), (72, 79, 68),
        (74, 70, 74), (75, 91, 11), (76, 72, 76), (77, 58, 45), (78, 126, 94), (79, 67, 63), (80, 81, 94), (81, 98, 22),
        (82, 80, 5), (83, 99, 19), (84, 93, 37), (85, 69, 90), (86, 94, 53), (87, 86, 69), (88, 22, 104), (89, 73, 105),
        (90, 89, 87), (91, 92, 21), (92, 18, 44), (94, 110, 94), (95, 12, 92), (96, 97, 6), (97, 114, 23), (99, 107, 38),
        (101, 108, 54), (102, 101, 70), (103, 96, 102), (104, 46, 14), (105, 104, 111), (107, 41, 27), (109, 43, 61), (110, 102, 108),
        (112, 127, 119), (113, 112, 7), (114, 113, 121), (115, 124, 123), (116, 100, 52), (117, 116, 71), (118, 119, 103), (119, 103, 126),
        (122, 32, 42), (123, 120, 119), (126, 118, 110), (127, 87, 124),
    ],
]
NRELAY = 4
NBUF = 1 + len(FIRST) + len(SECOND)


def holders():
    held = [{d: 0} for d in range(ND)]
    for n, edges in enumerate(FIRST):
        for _, there, tile in edges:
            held[there].setdefault(tile, 1 + n)
    source = np.zeros((len(SECOND), ND), np.int32)
    for n, edges in enumerate(SECOND):
        for here, _, tile in edges:
            source[n, here] = held[here][tile]
    for n, edges in enumerate(SECOND):
        for _, there, tile in edges:
            held[there].setdefault(tile, 1 + len(FIRST) + n)
    place = np.zeros((ND, 8), np.int32)
    for a in range(NR):
        for b in range(NC):
            for s in range(2):
                k = (a + b + s) % NR
                low = b < NR
                need = [
                    (k, b) if not low or k <= b else (b, k),
                    (b, k + NR) if low else (k, b) if k + NR <= b else (b - NR, k + NR),
                    (a, k) if a <= k else (k, a),
                    (a, k + NR),
                ]
                d = a * NC + b
                for kind, (r, c) in enumerate(need):
                    place[d, 4 * s + kind] = held[d][r * NC + c]
    return source, place


def slot_table(occupancy):
    i = np.arange(NB)
    before_col = (i[:, None] // CB == i[None, :] // CB) & (i[:, None] < i[None, :])
    panel = i[:, None] // CB == i[None, :] // CB
    before_row = (i[:, None] // CB % NR == i[None, :] // CB % NR) & (i[None, :] < i[:, None])
    occ = occupancy.astype(jnp.float32)
    dot = functools.partial(jnp.dot, precision=lax.Precision.HIGHEST)
    rank = dot(occ, jnp.asarray(before_col, jnp.float32)) + dot(
        jnp.asarray(before_row, jnp.float32), dot(occ, jnp.asarray(panel, jnp.float32))
    )
    return jnp.where(occupancy == 1, rank.astype(jnp.int32), -1)


def pick_kernel(source, lists, *refs):
    bufs, outs, sems = refs[: 1 + NRELAY], refs[1 + NRELAY : -1], refs[-1]
    here = lax.axis_index("row") * NC + lax.axis_index("col")
    for n, out in enumerate(outs):
        which = source[n * ND + here]
        for i in range(1 + NRELAY):

            @pl.when(which == i)
            def _():
                pltpu.make_async_copy(bufs[i], out, sems.at[n]).start()

    for n, out in enumerate(outs):
        pltpu.make_async_copy(bufs[0], out, sems.at[n]).wait()


def index_kernel(table, place, lists, blank, used):
    a = lax.axis_index("row")
    b = lax.axis_index("col")
    here = a * NC + b
    blank[...] = jnp.zeros_like(blank)

    def clear_used(t, carry):
        used[t] = 0
        return carry

    lax.fori_loop(0, 80, clear_used, 0)

    def step(t, n):
        s = t // 32
        kk = lax.rem(t // 2, 16)
        i = lax.rem(t, 2)
        half = kk // CB
        k = lax.rem(a + b + s, NR)
        inner = (half * NR + k) * CB + lax.rem(kk, CB)
        row = a * CB + i
        lslot = table[jnp.minimum(row, inner), jnp.maximum(row, inner)]
        lplace = (4 * s + 2 + half) * SLOTS + lslot
        turned = jnp.where(row > inner, 1, 0)

        def one_col(j, n0):
            n, fresh = n0
            col = b * CB + j
            rslot = table[jnp.minimum(inner, col), jnp.maximum(inner, col)]
            rplace = (4 * s + half) * SLOTS + rslot
            hit = rslot >= 0

            @pl.when(hit)
            def _():
                first = jnp.where(used[64 + i * CB + j] == 0, 1, 0)
                lists[n] = (
                    lplace
                    + (rplace << 6)
                    + ((i * CB + j) << 12)
                    + (turned << 16)
                    + (jnp.where(inner > col, 1, 0) << 17)
                    + (fresh << 18)
                    + (first << 19)
                )
                used[64 + i * CB + j] = 1
                used[lplace] = 1
                used[rplace] = 1

            one = jnp.where(hit, 1, 0)
            return n + one, fresh * (1 - one)

        return lax.cond(lslot >= 0, lambda m: lax.fori_loop(0, CB, one_col, (m, 1))[0], lambda m: m, n)

    count = lax.fori_loop(0, 64, step, 1)
    lists[0] = count
    for t in range(16):
        lists[FETCH + 112 + t] = used[64 + t]

    def by_buffer(buf, n):
        lists[FETCH + buf] = n

        def by_kind(kind, n):
            def by_slot(slot, n):
                @pl.when(used[kind * SLOTS + slot] == 1)
                def _():
                    lists[FETCH + n] = kind * SLOTS + slot

                return n + used[kind * SLOTS + slot]

            return lax.cond(
                place[here * 8 + kind] == buf, lambda m: lax.fori_loop(0, SLOTS, by_slot, m), lambda m: m, n
            )

        return lax.fori_loop(0, 8, by_kind, n)

    lists[FETCH + NBUF] = lax.fori_loop(0, NBUF, by_buffer, 32)


def product_kernel(lists, *refs):
    bufs = refs[:NBUF]
    blank, out, tiles, left, acc, sems, out_sems = refs[NBUF:]
    for n, buf in enumerate(bufs):

        def start(q, carry):
            t = lists[FETCH + q]
            pltpu.make_async_copy(buf.at[lax.rem(t, SLOTS)], tiles.at[t], sems.at[t]).start()
            return carry

        lax.fori_loop(lists[FETCH + n], lists[FETCH + n + 1], start, 0)

    def finish(q, carry):
        t = lists[FETCH + q]
        pltpu.make_async_copy(bufs[0].at[0], tiles.at[t], sems.at[t]).wait()
        return carry

    lax.fori_loop(32, lists[FETCH + NBUF], finish, 0)

    def product(q, carry):
        code = lists[q]
        lt = tiles.at[code & 63]
        rt = tiles.at[(code >> 6) & 63]
        to = acc.at[(code >> 12) & 15]

        @pl.when(((code >> 18) & 1) == 1)
        def _():
            @pl.when(((code >> 16) & 1) == 0)
            def _():
                left[...] = lt[...]

            @pl.when(((code >> 16) & 1) == 1)
            def _():
                left[...] = lt[...].T

        @pl.when(((code >> 19) & 1) == 1)
        def _():
            to[...] = jnp.zeros_like(to)

        @pl.when(((code >> 17) & 1) == 0)
        def _():
            to[...] += jnp.dot(left[...], rt[...], preferred_element_type=jnp.float32)

        @pl.when(((code >> 17) & 1) == 1)
        def _():
            to[...] += lax.dot_general(
                left[...], rt[...], (((1,), (1,)), ((), ())), preferred_element_type=jnp.float32
            )

        return carry

    lax.fori_loop(1, lists[0], product, 0)

    def copy_out(t):
        return pltpu.make_async_copy(
            acc.at[t], out.at[pl.ds(t // CB * BS, BS), pl.ds(t % CB * BS, BS)], out_sems.at[t]
        )

    for t in range(16):

        @pl.when(lists[FETCH + 112 + t] == 1)
        def _():
            copy_out(t).start()

    for t in range(16):

        @pl.when(lists[FETCH + 112 + t] == 1)
        def _():
            copy_out(t).wait()


def tile_shape():
    return jax.ShapeDtypeStruct((SLOTS, BS, BS), jnp.bfloat16)


SMEM = pl.BlockSpec(memory_space=pltpu.SMEM)
ANY = pl.BlockSpec(memory_space=pl.ANY)


def local(occupancy, stored):
    own = stored.reshape(SLOTS, BS, BS)
    source, place = holders()
    bufs = [own]
    for edges in FIRST:
        bufs.append(lax.ppermute(own, ("row", "col"), [(u, v) for u, v, _ in edges]))
    lists, blank = pl.pallas_call(
        index_kernel,
        out_shape=(
            jax.ShapeDtypeStruct((FETCH + 128,), jnp.int32),
            jax.ShapeDtypeStruct((SR * BS, CB * BS), jnp.float32),
        ),
        in_specs=[SMEM, SMEM],
        out_specs=(SMEM, pl.BlockSpec(memory_space=pltpu.VMEM)),
        scratch_shapes=[pltpu.SMEM((80,), jnp.int32)],
        cost_estimate=pl.CostEstimate(flops=10**9, bytes_accessed=4 * MIB, transcendentals=0),
        name="index",
    )(slot_table(occupancy), jnp.asarray(place.reshape(-1)))
    flat_source = jnp.asarray(source.reshape(-1))
    sends = pl.pallas_call(
        pick_kernel,
        out_shape=[tile_shape()] * len(SECOND),
        in_specs=[SMEM, SMEM] + [ANY] * (1 + NRELAY),
        out_specs=[pl.BlockSpec(memory_space=pltpu.VMEM)] * len(SECOND),
        scratch_shapes=[pltpu.SemaphoreType.DMA((len(SECOND),))],
        cost_estimate=pl.CostEstimate(flops=0, bytes_accessed=2 * MIB, transcendentals=0),
        name="pick",
    )(flat_source, lists, *bufs[: 1 + NRELAY])
    later = [
        lax.ppermute(send, ("row", "col"), [(u, v) for u, v, _ in edges])
        for send, edges in zip(sends, SECOND, strict=True)
    ]
    bufs += later
    return pl.pallas_call(
        product_kernel,
        out_shape=jax.ShapeDtypeStruct((SR * BS, CB * BS), jnp.float32),
        in_specs=[SMEM] + [ANY] * (NBUF + 1),
        out_specs=ANY,
        scratch_shapes=[
            pltpu.VMEM((64, BS, BS), jnp.bfloat16),
            pltpu.VMEM((BS, BS), jnp.bfloat16),
            pltpu.VMEM((16, BS, BS), jnp.float32),
            pltpu.SemaphoreType.DMA((64,)),
            pltpu.SemaphoreType.DMA((16,)),
        ],
        input_output_aliases={1 + NBUF: 0},
        compiler_params=pltpu.CompilerParams(vmem_limit_bytes=60 * MIB),
        cost_estimate=pl.CostEstimate(flops=10**9, bytes_accessed=12 * MIB, transcendentals=0),
        name="products",
    )(lists, *bufs, blank)


def solution(mesh):
    placed = (P(), P("row", "col", None, None, None))
    return jax.shard_map(
        local, mesh=mesh, in_specs=placed, out_specs=P("row", "col"), check_vma=False
    )
```

```python
import functools

import jax
import jax.numpy as jnp
import numpy as np
from jax import lax
from jax.experimental import pallas as pl
from jax.experimental.pallas import tpu as pltpu
from jax.sharding import PartitionSpec as P

BS = 256
CB = 8
SLOTS = 8
SR = 2
NB = 128
NR = 8
NC = 16
ND = NR * NC
MIB = 1024 * 1024
FETCH = 640

FIRST = [
    [
        (1, 9, 1), (3, 2, 3), (5, 4, 5), (11, 10, 11), (17, 16, 17), (18, 24, 18), (19, 18, 19), (20, 27, 20),
        (21, 20, 21), (22, 65, 22), (23, 81, 23), (28, 94, 28), (29, 28, 29), (30, 46, 30), (31, 30, 31), (35, 99, 35),
        (36, 41, 36), (38, 54, 38), (40, 37, 40), (43, 26, 43), (44, 33, 44), (46, 43, 46), (52, 116, 52), (53, 57, 53),
        (54, 50, 54), (55, 59, 55), (56, 52, 56), (58, 63, 58), (60, 124, 60), (69, 117, 69), (70, 86, 70), (71, 66, 71),
        (72, 56, 72), (73, 76, 73), (77, 73, 77), (85, 80, 85), (86, 88, 86), (90, 69, 90), (94, 29, 94), (95, 90, 95),
        (102, 103, 102), (103, 96, 103), (104, 105, 104), (105, 106, 105), (108, 109, 108), (111, 108, 111), (121, 89, 121), (124, 125, 124),
    ],
    [
        (1, 97, 1), (2, 82, 2), (3, 67, 3), (5, 90, 5), (6, 5, 6), (7, 23, 7), (8, 15, 8), (9, 8, 9),
        (10, 27, 10), (11, 75, 11), (12, 48, 12), (13, 72, 13), (14, 80, 14), (15, 120, 15), (17, 29, 17), (18, 38, 18),
        (19, 53, 19), (20, 33, 20), (21, 19, 21), (22, 107, 22), (23, 22, 23), (25, 16, 25), (27, 26, 27), (28, 41, 28),
        (29, 20, 29), (30, 89, 30), (31, 47, 31), (34, 114, 34), (35, 18, 35), (36, 100, 36), (37, 84, 37), (38, 35, 38),
        (39, 37, 39), (41, 9, 41), (42, 10, 42), (43, 32, 43), (44, 108, 44), (45, 93, 45), (46, 44, 46), (47, 63, 47),
        (52, 70, 52), (53, 49, 53), (54, 86, 54), (55, 116, 55), (56, 40, 56), (57, 61, 57), (58, 55, 58), (59, 56, 59),
        (60, 3, 60), (61, 57, 61), (62, 50, 62), (68, 64, 68), (69, 95, 69), (70, 102, 70), (71, 74, 71), (73, 69, 73),
        (74, 78, 74), (75, 11, 75), (76, 124, 76), (77, 65, 77), (78, 66, 78), (79, 36, 79), (85, 87, 85), (86, 81, 86),
        (87, 117, 87), (88, 42, 88), (89, 83, 89), (91, 94, 91), (92, 101, 92), (93, 13, 93), (94, 126, 94), (95, 21, 95),
        (102, 118, 102), (103, 104, 103), (104, 98, 104), (105, 54, 105), (106, 58, 106), (107, 109, 107), (110, 111, 110), (111, 30, 111),
        (119, 7, 119), (120, 113, 120), (121, 105, 121), (123, 115, 123), (124, 60, 124), (126, 119, 126),
    ],
    [
        (0, 8, 0), (1, 16, 1), (2, 45, 2), (3, 11, 3), (4, 12, 4), (5, 53, 5), (6, 96, 6), (9, 105, 9),
        (10, 1, 10), (11, 56, 11), (12, 76, 12), (13, 4, 13), (14, 30, 14), (15, 6, 15), (17, 113, 17), (18, 17, 18),
        (19, 26, 19), (20, 68, 20), (21, 83, 21), (22, 20, 22), (23, 121, 23), (24, 23, 24), (26, 24, 26), (27, 18, 27),
        (28, 19, 28), (29, 61, 29), (30, 29, 30), (31, 22, 31), (34, 39, 34), (35, 62, 35), (36, 70, 36), (37, 35, 37),
        (38, 43, 38), (39, 115, 39), (40, 98, 40), (41, 38, 41), (42, 32, 42), (43, 107, 43), (45, 58, 45), (46, 78, 46),
        (47, 36, 47), (51, 3, 51), (52, 48, 52), (53, 86, 53), (54, 101, 54), (55, 52, 55), (56, 67, 56), (57, 25, 57),
        (58, 10, 58), (59, 55, 59), (60, 49, 60), (61, 109, 61), (62, 47, 62), (63, 59, 63), (68, 71, 68), (69, 65, 69),
        (70, 66, 70), (71, 124, 71), (72, 75, 72), (73, 41, 73), (74, 84, 74), (75, 79, 75), (76, 64, 76), (77, 28, 77),
        (78, 44, 78), (79, 60, 79), (85, 117, 85), (86, 21, 86), (87, 82, 87), (88, 91, 88), (89, 73, 89), (90, 42, 90),
        (91, 27, 91), (93, 80, 93), (94, 5, 94), (95, 81, 95), (102, 106, 102), (103, 119, 103), (105, 99, 105), (106, 74, 106),
        (107, 100, 107), (108, 102, 108), (109, 111, 109), (110, 126, 110), (111, 97, 111), (119, 120, 119), (120, 7, 120), (121, 114, 121),
        (122, 123, 122), (123, 116, 123), (124, 87, 124), (125, 118, 125), (126, 14, 126), (127, 112, 127),
    ],
    [
        (0, 12, 0), (1, 63, 1), (2, 10, 2), (3, 60, 3), (4, 64, 4), (5, 37, 5), (6, 14, 6), (7, 113, 7),
        (8, 7, 8), (9, 0, 9), (10, 40, 10), (11, 2, 11), (12, 11, 12), (13, 45, 13), (14, 6, 14), (15, 124, 15),
        (17, 1, 17), (18, 47, 18), (19, 83, 19), (20, 19, 20), (21, 49, 21), (22, 28, 22), (23, 97, 23), (24, 31, 24),
        (25, 121, 25), (26, 9, 26), (27, 91, 27), (28, 27, 28), (29, 77, 29), (30, 21, 30), (34, 32, 34), (35, 54, 35),
        (36, 33, 36), (37, 43, 37), (38, 100, 38), (39, 36, 39), (40, 24, 40), (41, 98, 41), (42, 39, 42), (43, 18, 43),
        (44, 41, 44), (45, 127, 45), (46, 35, 46), (47, 44, 47), (51, 48, 51), (52, 57, 52), (53, 85, 53), (54, 58, 54),
        (55, 71, 55), (56, 61, 56), (57, 53, 57), (58, 115, 58), (59, 123, 59), (60, 56, 60), (61, 50, 61), (62, 94, 62),
        (63, 79, 63), (68, 72, 68), (69, 20, 69), (70, 73, 70), (71, 52, 71), (72, 76, 72), (73, 84, 73), (74, 26, 74),
        (75, 70, 75), (76, 8, 76), (77, 109, 77), (78, 74, 78), (79, 67, 79), (85, 5, 85), (86, 103, 86), (87, 90, 87),
        (88, 82, 88), (89, 69, 89), (90, 92, 90), (91, 101, 91), (92, 95, 92), (93, 88, 93), (94, 81, 94), (95, 29, 95),
        (102, 96, 102), (103, 22, 103), (104, 38, 104), (105, 89, 105), (106, 99, 106), (107, 86, 107), (108, 110, 108), (109, 13, 109),
        (110, 118, 110), (111, 104, 111), (119, 112, 119), (121, 122, 121), (122, 114, 122), (123, 75, 123), (124, 117, 124), (125, 126, 125),
        (127, 15, 127),
    ],
]
SECOND = [
    [
        (0, 7, 0), (1, 16, 10), (3, 53, 3), (4, 48, 4), (5, 64, 5), (6, 22, 6), (7, 15, 7), (8, 4, 76),
        (9, 1, 26), (10, 9, 2), (11, 116, 75), (12, 60, 12), (13, 95, 93), (14, 13, 14), (15, 0, 8), (16, 31, 25),
        (17, 114, 18), (18, 33, 27), (19, 27, 21), (20, 87, 69), (21, 5, 86), (22, 21, 31), (23, 30, 23), (24, 17, 26),
        (25, 23, 25), (26, 25, 19), (27, 77, 20), (28, 12, 77), (29, 24, 17), (30, 81, 30), (31, 29, 31), (32, 40, 43),
        (33, 18, 36), (34, 2, 34), (35, 41, 35), (36, 52, 79), (37, 45, 39), (38, 46, 41), (39, 122, 42), (40, 106, 10),
        (41, 26, 44), (42, 37, 88), (43, 108, 38), (44, 74, 47), (45, 38, 2), (46, 62, 30), (47, 105, 31), (48, 78, 52),
        (49, 35, 53), (50, 19, 61), (52, 36, 71), (53, 54, 57), (54, 50, 38), (56, 32, 11), (57, 58, 61), (58, 42, 45),
        (59, 63, 59), (60, 44, 79), (61, 49, 61), (62, 59, 62), (63, 51, 63), (64, 76, 4), (66, 65, 78), (67, 83, 3),
        (68, 69, 20), (69, 72, 69), (70, 100, 75), (71, 67, 55), (72, 68, 72), (73, 57, 89), (74, 70, 74), (75, 91, 11),
        (76, 79, 76), (77, 73, 29), (78, 66, 46), (79, 75, 79), (80, 96, 14), (81, 89, 94), (82, 126, 87), (83, 99, 19),
        (84, 93, 37), (85, 101, 53), (86, 20, 70), (87, 71, 124), (88, 90, 88), (89, 84, 89), (90, 80, 5), (91, 86, 91),
        (92, 28, 92), (93, 34, 45), (94, 88, 94), (95, 94, 92), (96, 98, 6), (97, 113, 1), (98, 97, 104), (99, 115, 35),
        (100, 107, 38), (101, 109, 54), (102, 110, 70), (103, 118, 86), (105, 39, 121), (106, 111, 102), (107, 123, 43), (108, 92, 44),
        (109, 43, 61), (110, 104, 110), (111, 127, 111), (113, 121, 7), (114, 55, 122), (115, 82, 39), (116, 3, 52), (117, 125, 87),
        (118, 6, 102), (119, 103, 126), (120, 112, 15), (123, 124, 123), (124, 117, 71), (126, 14, 110), (127, 119, 127),
    ],
    [
        (0, 112, 0), (1, 32, 10), (3, 19, 60), (4, 11, 4), (5, 13, 5), (6, 5, 14), (7, 23, 120), (8, 12, 76),
        (9, 122, 26), (10, 2, 42), (11, 72, 12), (12, 4, 12), (13, 29, 109), (14, 30, 126), (15, 7, 127), (16, 22, 1),
        (17, 1, 18), (18, 33, 19), (19, 49, 28), (20, 27, 29), (22, 89, 31), (23, 39, 23), (24, 25, 18), (25, 9, 25),
        (26, 10, 43), (27, 90, 10), (28, 20, 77), (30, 46, 14), (31, 81, 31), (32, 41, 43), (33, 18, 44), (35, 50, 46),
        (36, 82, 47), (37, 44, 39), (38, 36, 38), (39, 55, 39), (40, 24, 10), (41, 42, 36), (42, 47, 42), (43, 92, 37),
        (44, 66, 47), (45, 37, 2), (47, 97, 31), (48, 115, 51), (49, 53, 21), (50, 35, 61), (51, 63, 51), (53, 62, 19),
        (54, 38, 105), (55, 3, 59), (56, 52, 72), (57, 58, 53), (58, 54, 106), (59, 60, 55), (60, 61, 3), (61, 57, 29),
        (63, 31, 1), (64, 68, 4), (65, 98, 22), (66, 65, 70), (67, 48, 3), (68, 76, 20), (69, 85, 90), (70, 78, 36),
        (71, 116, 71), (72, 80, 13), (73, 74, 70), (74, 75, 71), (75, 71, 123), (76, 64, 12), (77, 125, 77), (78, 94, 78),
        (79, 67, 63), (80, 95, 85), (81, 113, 23), (82, 16, 2), (83, 91, 21), (84, 69, 74), (85, 88, 85), (86, 70, 107),
        (87, 21, 87), (88, 111, 86), (89, 73, 30), (90, 83, 5), (91, 107, 27), (92, 86, 92), (93, 77, 45), (94, 93, 91),
        (95, 87, 92), (96, 105, 6), (97, 114, 23), (99, 40, 35), (100, 84, 36), (101, 117, 92), (102, 101, 70), (103, 110, 86),
        (104, 106, 104), (105, 121, 9), (106, 108, 106), (107, 43, 107), (108, 14, 111), (109, 102, 109), (110, 28, 108), (111, 103, 109),
        (112, 120, 127), (115, 99, 58), (116, 100, 52), (117, 118, 87), (118, 6, 110), (119, 127, 103), (120, 104, 15), (123, 59, 123),
        (124, 96, 15), (126, 45, 125),
    ],
    [
        (1, 0, 1), (2, 48, 11), (3, 27, 60), (4, 75, 4), (5, 106, 6), (6, 38, 6), (7, 14, 7), (8, 120, 8),
        (9, 24, 9), (10, 26, 58), (11, 56, 12), (12, 3, 12), (13, 5, 93), (14, 13, 6), (15, 112, 8), (16, 1, 25),
        (17, 23, 17), (18, 2, 35), (19, 92, 21), (20, 86, 69), (21, 28, 21), (22, 54, 22), (23, 21, 23), (24, 8, 24),
        (25, 41, 57), (26, 16, 26), (27, 43, 91), (28, 76, 28), (29, 31, 17), (30, 6, 111), (31, 97, 24), (32, 114, 42),
        (33, 34, 36), (35, 50, 37), (36, 90, 47), (37, 122, 39), (38, 22, 104), (39, 40, 34), (40, 45, 40), (41, 42, 44),
        (42, 84, 90), (43, 44, 38), (44, 36, 78), (45, 32, 2), (46, 65, 30), (47, 46, 18), (48, 19, 52), (49, 69, 21),
        (50, 35, 62), (53, 61, 19), (54, 70, 38), (55, 51, 55), (56, 57, 60), (57, 79, 52), (58, 100, 106), (59, 124, 55),
        (60, 52, 3), (61, 49, 29), (62, 58, 62), (63, 30, 1), (64, 71, 76), (65, 81, 22), (67, 83, 56), (69, 53, 89),
        (70, 77, 36), (71, 4, 68), (72, 64, 13), (73, 109, 70), (74, 20, 78), (75, 67, 72), (76, 72, 76), (78, 62, 46),
        (79, 95, 79), (80, 87, 93), (81, 82, 95), (82, 98, 2), (83, 17, 19), (84, 85, 37), (86, 94, 53), (87, 37, 87),
        (89, 91, 89), (90, 89, 95), (91, 25, 27), (93, 125, 93), (94, 110, 94), (95, 12, 92), (96, 80, 6), (98, 47, 41),
        (99, 33, 35), (100, 66, 38), (101, 108, 54), (102, 104, 102), (104, 88, 104), (105, 73, 105), (107, 99, 22), (108, 101, 108),
        (109, 93, 61), (110, 103, 110), (111, 118, 109), (112, 127, 119), (113, 96, 7), (114, 39, 122), (115, 123, 39), (116, 55, 123),
        (118, 117, 125), (119, 126, 103), (121, 113, 25), (122, 74, 122), (123, 115, 59), (124, 116, 76), (126, 29, 125),
    ],
    [
        (0, 16, 9), (1, 2, 10), (2, 1, 2), (3, 11, 60), (4, 5, 13), (5, 12, 5), (6, 7, 15), (7, 120, 7),
        (9, 25, 41), (10, 9, 10), (11, 10, 3), (12, 15, 0), (13, 61, 13), (15, 31, 15), (17, 98, 18), (18, 17, 27),
        (19, 18, 28), (20, 21, 22), (21, 37, 95), (22, 6, 103), (23, 29, 23), (24, 106, 26), (25, 83, 57), (26, 42, 74),
        (27, 26, 28), (28, 33, 28), (29, 28, 30), (30, 22, 111), (31, 30, 24), (33, 34, 44), (34, 47, 34), (35, 36, 46),
        (37, 38, 40), (38, 39, 41), (40, 46, 40), (41, 57, 28), (42, 40, 42), (43, 58, 46), (44, 110, 78), (47, 45, 47),
        (48, 49, 52), (49, 50, 53), (50, 51, 62), (51, 55, 51), (52, 71, 52), (53, 54, 19), (54, 35, 54), (56, 48, 59),
        (57, 56, 52), (58, 43, 45), (59, 52, 63), (61, 62, 57), (63, 60, 63), (64, 3, 4), (65, 64, 77), (66, 67, 71),
        (67, 74, 79), (68, 116, 68), (69, 73, 69), (70, 69, 36), (71, 87, 71), (72, 88, 13), (73, 4, 77), (74, 70, 106),
        (77, 65, 29), (78, 77, 74), (79, 75, 63), (80, 117, 93), (81, 80, 94), (82, 81, 87), (83, 84, 21), (84, 100, 74),
        (85, 19, 53), (86, 93, 53), (87, 89, 87), (88, 72, 88), (89, 92, 89), (90, 82, 5), (91, 53, 88), (94, 78, 62),
        (95, 111, 95), (96, 97, 103), (97, 23, 1), (98, 114, 41), (99, 32, 35), (100, 99, 38), (101, 85, 91), (102, 86, 108),
        (103, 102, 86), (104, 105, 111), (106, 107, 106), (107, 59, 107), (109, 27, 61), (110, 44, 108), (111, 96, 110), (113, 112, 120),
        (114, 113, 121), (115, 66, 39), (116, 115, 55), (117, 101, 69), (118, 103, 125), (119, 118, 103), (120, 104, 120), (121, 122, 23),
        (122, 90, 122), (124, 108, 60), (126, 13, 94),
    ],
    [
        (0, 1, 9), (2, 3, 11), (3, 32, 3), (4, 52, 4), (5, 21, 94), (7, 6, 7), (9, 8, 1), (11, 27, 75),
        (13, 12, 13), (15, 14, 15), (17, 16, 18), (18, 2, 43), (19, 18, 20), (20, 4, 69), (21, 20, 30), (22, 38, 22),
        (23, 22, 24), (24, 25, 26), (25, 24, 25), (27, 26, 20), (28, 29, 22), (29, 45, 95), (30, 88, 14), (31, 113, 24),
        (32, 33, 43), (33, 49, 20), (35, 34, 37), (36, 37, 47), (38, 39, 18), (41, 57, 73), (42, 58, 90), (43, 42, 37),
        (44, 28, 78), (45, 46, 2), (47, 43, 62), (48, 56, 51), (49, 48, 60), (50, 51, 54), (52, 53, 56), (53, 99, 57),
        (54, 55, 35), (55, 54, 58), (56, 40, 11), (58, 59, 54), (59, 11, 59), (60, 44, 124), (61, 60, 56), (62, 63, 35),
        (63, 62, 58), (64, 67, 4), (65, 64, 69), (67, 66, 79), (68, 84, 20), (69, 68, 73), (70, 71, 75), (71, 123, 55),
        (72, 79, 68), (73, 72, 77), (74, 73, 78), (76, 77, 73), (77, 19, 29), (78, 74, 46), (79, 78, 75), (80, 104, 14),
        (81, 80, 86), (82, 83, 88), (83, 65, 21), (84, 69, 37), (86, 70, 54), (87, 103, 87), (88, 89, 86), (89, 23, 121),
        (90, 91, 5), (91, 41, 27), (92, 93, 90), (93, 35, 45), (94, 92, 28), (95, 94, 69), (96, 97, 6), (97, 96, 111),
        (98, 82, 40), (99, 98, 105), (100, 101, 107), (101, 100, 54), (102, 36, 70), (104, 105, 103), (106, 107, 105), (107, 106, 22),
        (109, 108, 107), (111, 110, 109), (113, 112, 7), (114, 115, 122), (115, 114, 39), (117, 116, 124), (118, 87, 125), (119, 118, 126),
        (120, 121, 120), (124, 125, 71), (126, 127, 126), (127, 50, 45),
    ],
]
NRELAY = 4
NBUF = 1 + len(FIRST) + len(SECOND)


def holders():
    held = [{d: 0} for d in range(ND)]
    for n, edges in enumerate(FIRST):
        for _, there, tile in edges:
            held[there].setdefault(tile, 1 + n)
    source = np.zeros((len(SECOND), ND), np.int32)
    for n, edges in enumerate(SECOND):
        for here, _, tile in edges:
            source[n, here] = held[here][tile]
    for n, edges in enumerate(SECOND):
        for _, there, tile in edges:
            held[there].setdefault(tile, 1 + len(FIRST) + n)
    place = np.zeros((ND, 8), np.int32)
    for a in range(NR):
        for b in range(NC):
            for s in range(2):
                k = (a + b + s) % NR
                low = b < NR
                need = [
                    (k, b) if not low or k <= b else (b, k),
                    (b, k + NR) if low else (k, b) if k + NR <= b else (b - NR, k + NR),
                    (a, k) if a <= k else (k, a),
                    (a, k + NR),
                ]
                d = a * NC + b
                for kind, (r, c) in enumerate(need):
                    place[d, 4 * s + kind] = held[d][r * NC + c]
    return source, place


def slot_table(occupancy):
    i = np.arange(NB)
    before_col = (i[:, None] // CB == i[None, :] // CB) & (i[:, None] < i[None, :])
    panel = i[:, None] // CB == i[None, :] // CB
    before_row = (i[:, None] // CB % NR == i[None, :] // CB % NR) & (i[None, :] < i[:, None])
    occ = occupancy.astype(jnp.float32)
    dot = functools.partial(jnp.dot, precision=lax.Precision.HIGHEST)
    rank = dot(occ, jnp.asarray(before_col, jnp.float32)) + dot(
        jnp.asarray(before_row, jnp.float32), dot(occ, jnp.asarray(panel, jnp.float32))
    )
    return jnp.where(occupancy == 1, rank.astype(jnp.int32), -1)


def pick_kernel(source, lists, *refs):
    bufs, outs, sems = refs[: 1 + NRELAY], refs[1 + NRELAY : -1], refs[-1]
    here = lax.axis_index("row") * NC + lax.axis_index("col")
    for n, out in enumerate(outs):
        which = source[n * ND + here]
        for i in range(1 + NRELAY):

            @pl.when(which == i)
            def _():
                pltpu.make_async_copy(bufs[i], out, sems.at[n]).start()

    for n, out in enumerate(outs):
        pltpu.make_async_copy(bufs[0], out, sems.at[n]).wait()


def index_kernel(table, place, lists, blank, used):
    a = lax.axis_index("row")
    b = lax.axis_index("col")
    here = a * NC + b
    blank[...] = jnp.zeros_like(blank)

    def clear_used(t, carry):
        used[t] = 0
        return carry

    lax.fori_loop(0, 80, clear_used, 0)

    def step(t, n):
        s = t // 32
        kk = lax.rem(t // 2, 16)
        i = lax.rem(t, 2)
        half = kk // CB
        k = lax.rem(a + b + s, NR)
        inner = (half * NR + k) * CB + lax.rem(kk, CB)
        row = a * CB + i
        lslot = table[jnp.minimum(row, inner), jnp.maximum(row, inner)]
        lplace = (4 * s + 2 + half) * SLOTS + lslot
        turned = jnp.where(row > inner, 1, 0)

        def one_col(j, n0):
            n, fresh = n0
            col = b * CB + j
            rslot = table[jnp.minimum(inner, col), jnp.maximum(inner, col)]
            rplace = (4 * s + half) * SLOTS + rslot
            hit = rslot >= 0

            @pl.when(hit)
            def _():
                first = jnp.where(used[64 + i * CB + j] == 0, 1, 0)
                lists[n] = (
                    lplace
                    + (rplace << 6)
                    + ((i * CB + j) << 12)
                    + (turned << 16)
                    + (jnp.where(inner > col, 1, 0) << 17)
                    + (fresh << 18)
                    + (first << 19)
                )
                used[64 + i * CB + j] = 1
                used[lplace] = 1
                used[rplace] = 1

            one = jnp.where(hit, 1, 0)
            return n + one, fresh * (1 - one)

        return lax.cond(lslot >= 0, lambda m: lax.fori_loop(0, CB, one_col, (m, 1))[0], lambda m: m, n)

    count = lax.fori_loop(0, 64, step, 1)
    lists[0] = count
    for t in range(16):
        lists[FETCH + 112 + t] = used[64 + t]

    def by_buffer(buf, n):
        lists[FETCH + buf] = n

        def by_kind(kind, n):
            def by_slot(slot, n):
                @pl.when(used[kind * SLOTS + slot] == 1)
                def _():
                    lists[FETCH + n] = kind * SLOTS + slot

                return n + used[kind * SLOTS + slot]

            return lax.cond(
                place[here * 8 + kind] == buf, lambda m: lax.fori_loop(0, SLOTS, by_slot, m), lambda m: m, n
            )

        return lax.fori_loop(0, 8, by_kind, n)

    lists[FETCH + NBUF] = lax.fori_loop(0, NBUF, by_buffer, 32)


def product_kernel(lists, *refs):
    bufs = refs[:NBUF]
    blank, out, tiles, left, acc, sems, out_sems = refs[NBUF:]
    for n, buf in enumerate(bufs):

        def start(q, carry):
            t = lists[FETCH + q]
            pltpu.make_async_copy(buf.at[lax.rem(t, SLOTS)], tiles.at[t], sems.at[t]).start()
            return carry

        lax.fori_loop(lists[FETCH + n], lists[FETCH + n + 1], start, 0)

    def finish(q, carry):
        t = lists[FETCH + q]
        pltpu.make_async_copy(bufs[0].at[0], tiles.at[t], sems.at[t]).wait()
        return carry

    lax.fori_loop(32, lists[FETCH + NBUF], finish, 0)

    def product(q, carry):
        code = lists[q]
        lt = tiles.at[code & 63]
        rt = tiles.at[(code >> 6) & 63]
        to = acc.at[(code >> 12) & 15]

        @pl.when(((code >> 18) & 1) == 1)
        def _():
            @pl.when(((code >> 16) & 1) == 0)
            def _():
                left[...] = lt[...]

            @pl.when(((code >> 16) & 1) == 1)
            def _():
                left[...] = lt[...].T

        @pl.when(((code >> 19) & 1) == 1)
        def _():
            to[...] = jnp.zeros_like(to)

        @pl.when(((code >> 17) & 1) == 0)
        def _():
            to[...] += jnp.dot(left[...], rt[...], preferred_element_type=jnp.float32)

        @pl.when(((code >> 17) & 1) == 1)
        def _():
            to[...] += lax.dot_general(
                left[...], rt[...], (((1,), (1,)), ((), ())), preferred_element_type=jnp.float32
            )

        return carry

    lax.fori_loop(1, lists[0], product, 0)

    def copy_out(t):
        return pltpu.make_async_copy(
            acc.at[t], out.at[pl.ds(t // CB * BS, BS), pl.ds(t % CB * BS, BS)], out_sems.at[t]
        )

    for t in range(16):

        @pl.when(lists[FETCH + 112 + t] == 1)
        def _():
            copy_out(t).start()

    for t in range(16):

        @pl.when(lists[FETCH + 112 + t] == 1)
        def _():
            copy_out(t).wait()


def tile_shape():
    return jax.ShapeDtypeStruct((SLOTS, BS, BS), jnp.bfloat16)


SMEM = pl.BlockSpec(memory_space=pltpu.SMEM)
ANY = pl.BlockSpec(memory_space=pl.ANY)


def local(occupancy, stored):
    own = stored.reshape(SLOTS, BS, BS)
    source, place = holders()
    bufs = [own]
    for edges in FIRST:
        bufs.append(lax.ppermute(own, ("row", "col"), [(u, v) for u, v, _ in edges]))
    lists, blank = pl.pallas_call(
        index_kernel,
        out_shape=(
            jax.ShapeDtypeStruct((FETCH + 128,), jnp.int32),
            jax.ShapeDtypeStruct((SR * BS, CB * BS), jnp.float32),
        ),
        in_specs=[SMEM, SMEM],
        out_specs=(SMEM, pl.BlockSpec(memory_space=pltpu.VMEM)),
        scratch_shapes=[pltpu.SMEM((80,), jnp.int32)],
        cost_estimate=pl.CostEstimate(flops=10**9, bytes_accessed=4 * MIB, transcendentals=0),
        name="index",
    )(slot_table(occupancy), jnp.asarray(place.reshape(-1)))
    flat_source = jnp.asarray(source.reshape(-1))
    sends = pl.pallas_call(
        pick_kernel,
        out_shape=[pltpu.VMEM((SLOTS, BS, BS), jnp.bfloat16)] * len(SECOND),
        in_specs=[SMEM, SMEM] + [ANY] * (1 + NRELAY),
        out_specs=[pl.BlockSpec(memory_space=pltpu.VMEM)] * len(SECOND),
        compiler_params=pltpu.CompilerParams(vmem_limit_bytes=16 * MIB),
        scratch_shapes=[pltpu.SemaphoreType.DMA((len(SECOND),))],
        cost_estimate=pl.CostEstimate(flops=0, bytes_accessed=2 * MIB, transcendentals=0),
        name="pick",
    )(flat_source, lists, *bufs[: 1 + NRELAY])
    later = [
        lax.ppermute(send, ("row", "col"), [(u, v) for u, v, _ in edges])
        for send, edges in zip(sends, SECOND, strict=True)
    ]
    bufs += later
    return pl.pallas_call(
        product_kernel,
        out_shape=jax.ShapeDtypeStruct((SR * BS, CB * BS), jnp.float32),
        in_specs=[SMEM] + [ANY] * (NBUF + 1),
        out_specs=ANY,
        scratch_shapes=[
            pltpu.VMEM((64, BS, BS), jnp.bfloat16),
            pltpu.VMEM((BS, BS), jnp.bfloat16),
            pltpu.VMEM((16, BS, BS), jnp.float32),
            pltpu.SemaphoreType.DMA((64,)),
            pltpu.SemaphoreType.DMA((16,)),
        ],
        input_output_aliases={1 + NBUF: 0},
        compiler_params=pltpu.CompilerParams(vmem_limit_bytes=60 * MIB),
        cost_estimate=pl.CostEstimate(flops=10**9, bytes_accessed=12 * MIB, transcendentals=0),
        name="products",
    )(lists, *bufs, blank)


def solution(mesh):
    placed = (P(), P("row", "col", None, None, None))
    return jax.shard_map(
        local, mesh=mesh, in_specs=placed, out_specs=P("row", "col"), check_vma=False
    )
```

```python
import functools

import jax
import jax.numpy as jnp
import numpy as np
from jax import lax
from jax.experimental import pallas as pl
from jax.experimental.pallas import tpu as pltpu
from jax.sharding import PartitionSpec as P

BS = 256
CB = 8
SLOTS = 8
SR = 2
NB = 128
NR = 8
NC = 16
ND = NR * NC
MIB = 1024 * 1024
FETCH = 640

FIRST = [
    [
        (1, 9, 1), (3, 2, 3), (5, 4, 5), (9, 8, 9), (11, 10, 11), (17, 29, 17), (18, 17, 18), (19, 18, 19),
        (20, 33, 20), (21, 20, 21), (22, 107, 22), (23, 81, 23), (25, 16, 25), (28, 27, 28), (29, 28, 29), (30, 21, 30),
        (31, 30, 31), (35, 99, 35), (36, 41, 36), (38, 35, 38), (39, 115, 39), (40, 37, 40), (43, 26, 43), (46, 43, 46),
        (52, 116, 52), (53, 57, 53), (54, 101, 54), (55, 52, 55), (56, 61, 56), (58, 63, 58), (60, 56, 60), (62, 50, 62),
        (68, 64, 68), (69, 117, 69), (70, 86, 70), (71, 66, 71), (73, 84, 73), (76, 124, 76), (77, 109, 77), (85, 80, 85),
        (86, 103, 86), (87, 82, 87), (94, 5, 94), (95, 90, 95), (102, 118, 102), (103, 22, 103), (104, 105, 104), (105, 89, 105),
        (106, 58, 106), (108, 102, 108), (110, 111, 110), (111, 108, 111), (119, 7, 119), (121, 122, 121), (124, 60, 124),
    ],
    [
        (1, 97, 1), (2, 45, 2), (3, 11, 3), (5, 90, 5), (6, 14, 6), (7, 23, 7), (9, 0, 9), (10, 27, 10),
        (11, 2, 11), (12, 76, 12), (13, 4, 13), (14, 30, 14), (15, 6, 15), (17, 16, 17), (18, 24, 18), (19, 83, 19),
        (20, 19, 20), (21, 49, 21), (22, 20, 22), (23, 22, 23), (25, 121, 25), (26, 9, 26), (27, 18, 27), (28, 94, 28),
        (29, 61, 29), (30, 29, 30), (34, 39, 34), (35, 54, 35), (36, 33, 36), (37, 43, 37), (38, 100, 38), (40, 98, 40),
        (41, 38, 41), (42, 32, 42), (43, 107, 43), (44, 41, 44), (45, 127, 45), (46, 78, 46), (47, 36, 47), (51, 48, 51),
        (52, 70, 52), (53, 85, 53), (54, 58, 54), (55, 116, 55), (56, 40, 56), (57, 53, 57), (58, 10, 58), (59, 123, 59),
        (60, 124, 60), (61, 50, 61), (62, 47, 62), (69, 65, 69), (70, 66, 70), (71, 74, 71), (72, 56, 72), (73, 69, 73),
        (74, 26, 74), (75, 79, 75), (77, 28, 77), (78, 44, 78), (79, 67, 79), (85, 5, 85), (86, 21, 86), (87, 117, 87),
        (88, 91, 88), (89, 73, 89), (90, 92, 90), (91, 101, 91), (93, 80, 93), (94, 126, 94), (95, 81, 95), (102, 103, 102),
        (103, 96, 103), (105, 99, 105), (107, 86, 107), (108, 109, 108), (111, 104, 111), (119, 120, 119), (120, 113, 120), (121, 89, 121),
        (122, 114, 122), (123, 75, 123), (124, 87, 124), (125, 118, 125), (126, 119, 126),
    ],
    [
        (0, 12, 0), (1, 16, 1), (2, 10, 2), (3, 60, 3), (4, 64, 4), (5, 53, 5), (6, 96, 6), (8, 7, 8),
        (10, 1, 10), (11, 75, 11), (12, 11, 12), (13, 45, 13), (14, 80, 14), (15, 124, 15), (17, 113, 17), (18, 47, 18),
        (19, 26, 19), (20, 27, 20), (21, 83, 21), (22, 28, 22), (23, 121, 23), (24, 23, 24), (27, 91, 27), (28, 19, 28),
        (29, 77, 29), (30, 46, 30), (31, 22, 31), (34, 114, 34), (35, 18, 35), (36, 100, 36), (37, 35, 37), (38, 43, 38),
        (39, 37, 39), (40, 24, 40), (41, 98, 41), (42, 39, 42), (43, 32, 43), (44, 108, 44), (45, 93, 45), (46, 44, 46),
        (47, 63, 47), (51, 3, 51), (52, 48, 52), (53, 86, 53), (54, 50, 54), (55, 71, 55), (56, 67, 56), (57, 61, 57),
        (58, 55, 58), (59, 56, 59), (60, 49, 60), (61, 57, 61), (63, 59, 63), (68, 72, 68), (69, 20, 69), (70, 73, 70),
        (71, 52, 71), (72, 76, 72), (73, 41, 73), (74, 84, 74), (75, 70, 75), (76, 8, 76), (77, 65, 77), (78, 66, 78),
        (79, 36, 79), (85, 117, 85), (86, 88, 86), (88, 82, 88), (89, 69, 89), (90, 42, 90), (91, 94, 91), (92, 95, 92),
        (93, 13, 93), (94, 81, 94), (95, 29, 95), (102, 106, 102), (103, 119, 103), (104, 38, 104), (105, 54, 105), (106, 74, 106),
        (107, 109, 107), (109, 111, 109), (110, 118, 110), (111, 97, 111), (119, 112, 119), (121, 105, 121), (122, 123, 122), (123, 115, 123),
        (124, 125, 124), (125, 126, 125), (127, 15, 127),
    ],
    [
        (0, 8, 0), (1, 63, 1), (2, 82, 2), (3, 67, 3), (4, 12, 4), (5, 37, 5), (6, 5, 6), (7, 113, 7),
        (8, 15, 8), (9, 105, 9), (10, 40, 10), (11, 56, 11), (12, 48, 12), (13, 72, 13), (14, 6, 14), (15, 120, 15),
        (17, 1, 17), (18, 38, 18), (19, 53, 19), (20, 68, 20), (21, 19, 21), (22, 65, 22), (23, 97, 23), (24, 31, 24),
        (26, 24, 26), (27, 26, 27), (28, 41, 28), (29, 20, 29), (30, 89, 30), (31, 47, 31), (34, 32, 34), (35, 62, 35),
        (36, 70, 36), (37, 84, 37), (38, 54, 38), (39, 36, 39), (41, 9, 41), (42, 10, 42), (43, 18, 43), (44, 33, 44),
        (45, 58, 45), (46, 35, 46), (47, 44, 47), (52, 57, 52), (53, 49, 53), (54, 86, 54), (55, 59, 55), (56, 52, 56),
        (57, 25, 57), (58, 115, 58), (59, 55, 59), (60, 3, 60), (61, 109, 61), (62, 94, 62), (63, 79, 63), (68, 71, 68),
        (69, 95, 69), (70, 102, 70), (71, 124, 71), (72, 75, 72), (73, 76, 73), (74, 78, 74), (75, 11, 75), (76, 64, 76),
        (77, 73, 77), (78, 74, 78), (79, 60, 79), (85, 87, 85), (86, 81, 86), (87, 90, 87), (88, 42, 88), (89, 83, 89),
        (90, 69, 90), (91, 27, 91), (92, 101, 92), (93, 88, 93), (94, 29, 94), (95, 21, 95), (102, 96, 102), (103, 104, 103),
        (104, 98, 104), (105, 106, 105), (106, 99, 106), (107, 100, 107), (108, 110, 108), (109, 13, 109), (110, 126, 110), (111, 30, 111),
        (120, 7, 120), (121, 114, 121), (123, 116, 123), (124, 117, 124), (126, 14, 126), (127, 112, 127),
    ],
]
SECOND = [
    [
        (0, 112, 0), (1, 16, 10), (2, 48, 11), (3, 32, 3), (4, 11, 4), (5, 13, 5), (6, 22, 6), (7, 15, 7),
        (8, 4, 76), (9, 24, 9), (10, 9, 10), (11, 116, 75), (12, 3, 12), (13, 29, 109), (14, 30, 126), (15, 0, 8),
        (16, 31, 25), (17, 1, 18), (18, 2, 35), (19, 27, 21), (20, 87, 69), (21, 5, 86), (22, 21, 31), (23, 39, 23),
        (24, 17, 26), (25, 23, 25), (26, 25, 19), (27, 77, 20), (28, 33, 28), (30, 46, 14), (31, 81, 31), (32, 41, 43),
        (33, 18, 36), (35, 50, 46), (36, 82, 47), (37, 44, 39), (38, 36, 38), (39, 122, 42), (40, 45, 40), (41, 26, 44),
        (42, 47, 42), (43, 92, 37), (44, 74, 47), (46, 62, 30), (47, 43, 62), (48, 115, 51), (49, 53, 21), (50, 35, 61),
        (53, 61, 19), (54, 38, 105), (55, 54, 58), (56, 52, 72), (57, 79, 52), (58, 42, 45), (59, 63, 59), (61, 49, 61),
        (62, 58, 62), (63, 51, 63), (64, 68, 4), (65, 98, 22), (66, 65, 70), (67, 83, 3), (68, 84, 20), (69, 72, 69),
        (70, 78, 36), (71, 123, 55), (72, 88, 13), (73, 57, 89), (74, 20, 78), (75, 71, 123), (76, 64, 12), (77, 19, 29),
        (78, 94, 78), (79, 67, 63), (80, 95, 85), (81, 89, 94), (82, 126, 87), (83, 91, 21), (84, 69, 37), (85, 101, 53),
        (86, 70, 107), (87, 37, 87), (88, 111, 86), (89, 73, 30), (90, 80, 5), (91, 107, 27), (92, 86, 92), (93, 34, 45),
        (94, 93, 91), (95, 12, 92), (96, 105, 6), (97, 114, 23), (98, 97, 104), (99, 40, 35), (100, 66, 38), (101, 109, 54),
        (102, 110, 70), (103, 118, 86), (104, 106, 104), (105, 121, 9), (106, 108, 106), (107, 59, 107), (109, 102, 109), (110, 28, 108),
        (111, 127, 111), (112, 120, 127), (113, 96, 7), (114, 55, 122), (115, 99, 58), (116, 100, 52), (117, 125, 87), (118, 6, 110),
        (119, 103, 126), (120, 104, 15), (121, 113, 25), (122, 90, 122), (123, 124, 123), (124, 117, 71), (126, 14, 110), (127, 119, 127),
    ],
    [
        (0, 7, 0), (1, 32, 10), (3, 27, 60), (4, 75, 4), (5, 64, 5), (6, 5, 14), (7, 120, 7), (8, 12, 76),
        (9, 25, 41), (10, 26, 58), (11, 56, 12), (12, 4, 12), (13, 61, 13), (15, 112, 8), (16, 1, 25), (17, 23, 17),
        (18, 33, 27), (19, 49, 28), (20, 86, 69), (21, 37, 95), (22, 6, 103), (23, 30, 23), (24, 106, 26), (25, 9, 25),
        (26, 16, 26), (27, 90, 10), (28, 29, 22), (29, 24, 17), (30, 88, 14), (31, 97, 24), (32, 114, 42), (33, 18, 44),
        (34, 2, 34), (35, 36, 46), (36, 52, 79), (37, 45, 39), (38, 22, 104), (39, 40, 34), (40, 46, 40), (41, 42, 44),
        (42, 84, 90), (43, 108, 38), (44, 66, 47), (45, 38, 2), (47, 105, 31), (48, 78, 52), (49, 35, 53), (50, 19, 61),
        (53, 62, 19), (54, 50, 38), (55, 3, 59), (56, 48, 59), (57, 58, 53), (58, 54, 106), (59, 60, 55), (60, 44, 79),
        (61, 57, 29), (63, 31, 1), (64, 71, 76), (65, 81, 22), (66, 65, 78), (67, 83, 56), (68, 76, 20), (69, 73, 69),
        (70, 69, 36), (71, 67, 55), (72, 68, 72), (73, 109, 70), (74, 70, 106), (76, 79, 76), (77, 125, 77), (78, 74, 46),
        (79, 95, 79), (80, 96, 14), (81, 113, 23), (82, 98, 2), (83, 17, 19), (84, 100, 74), (86, 94, 53), (87, 21, 87),
        (88, 72, 88), (89, 91, 89), (90, 89, 95), (91, 53, 88), (92, 28, 92), (93, 77, 45), (94, 92, 28), (95, 87, 92),
        (96, 80, 6), (99, 115, 35), (100, 99, 38), (101, 85, 91), (102, 101, 70), (103, 110, 86), (105, 39, 121), (106, 111, 102),
        (107, 43, 107), (108, 14, 111), (109, 93, 61), (111, 103, 109), (112, 127, 119), (113, 121, 7), (115, 82, 39), (116, 55, 123),
        (117, 118, 87), (118, 117, 125), (119, 126, 103), (120, 104, 120), (121, 122, 23), (123, 59, 123), (124, 116, 76), (126, 13, 94),
    ],
    [
        (1, 2, 10), (3, 53, 3), (4, 48, 4), (5, 12, 5), (6, 38, 6), (7, 14, 7), (8, 120, 8), (9, 1, 26),
        (10, 9, 2), (11, 27, 75), (12, 60, 12), (13, 5, 93), (14, 13, 14), (15, 7, 127), (16, 22, 1), (17, 114, 18),
        (18, 17, 27), (19, 18, 28), (20, 21, 22), (21, 28, 21), (22, 89, 31), (23, 29, 23), (24, 25, 26), (25, 83, 57),
        (26, 42, 74), (27, 26, 28), (28, 76, 28), (29, 31, 17), (30, 81, 30), (31, 113, 24), (32, 40, 43), (33, 34, 44),
        (35, 41, 35), (36, 90, 47), (37, 122, 39), (38, 46, 41), (39, 55, 39), (40, 106, 10), (41, 57, 73), (42, 58, 90),
        (43, 44, 38), (44, 110, 78), (45, 37, 2), (47, 97, 31), (48, 19, 52), (49, 69, 21), (50, 35, 62), (51, 63, 51),
        (52, 36, 71), (53, 54, 57), (54, 70, 38), (55, 51, 55), (56, 32, 11), (58, 100, 106), (59, 124, 55), (60, 52, 3),
        (61, 49, 29), (62, 59, 62), (63, 30, 1), (64, 3, 4), (67, 66, 79), (68, 116, 68), (69, 85, 90), (70, 77, 36),
        (71, 87, 71), (72, 64, 13), (73, 4, 77), (74, 73, 78), (75, 67, 72), (76, 72, 76), (78, 62, 46), (79, 75, 79),
        (80, 117, 93), (81, 80, 94), (82, 16, 2), (83, 65, 21), (84, 93, 37), (86, 20, 70), (87, 71, 124), (89, 84, 89),
        (90, 82, 5), (91, 86, 91), (93, 125, 93), (94, 88, 94), (95, 111, 95), (96, 98, 6), (97, 23, 1), (98, 47, 41),
        (99, 33, 35), (100, 107, 38), (101, 108, 54), (102, 104, 102), (104, 105, 103), (107, 99, 22), (108, 92, 44), (109, 43, 61),
        (110, 103, 110), (111, 118, 109), (114, 39, 122), (115, 123, 39), (116, 115, 55), (117, 101, 69), (118, 6, 102), (119, 127, 103),
        (120, 112, 15), (122, 74, 122), (124, 96, 15), (126, 45, 125), (127, 50, 45),
    ],
    [
        (0, 16, 9), (1, 0, 1), (2, 1, 2), (3, 19, 60), (4, 52, 4), (5, 106, 6), (7, 6, 7), (9, 122, 26),
        (10, 2, 42), (11, 72, 12), (12, 15, 0), (13, 95, 93), (14, 13, 6), (15, 31, 15), (17, 98, 18), (18, 33, 19),
        (19, 92, 21), (20, 4, 69), (21, 20, 30), (22, 38, 22), (23, 21, 23), (24, 8, 24), (25, 41, 57), (26, 10, 43),
        (27, 26, 20), (28, 12, 77), (29, 28, 30), (30, 22, 111), (31, 30, 24), (33, 49, 20), (34, 47, 34), (35, 34, 37),
        (38, 39, 18), (40, 24, 10), (41, 57, 28), (42, 37, 88), (43, 42, 37), (44, 36, 78), (45, 46, 2), (47, 45, 47),
        (48, 56, 51), (49, 50, 53), (50, 51, 62), (52, 71, 52), (53, 54, 19), (54, 55, 35), (56, 40, 11), (57, 58, 61),
        (58, 43, 45), (59, 11, 59), (60, 44, 124), (61, 62, 57), (63, 60, 63), (64, 67, 4), (65, 64, 69), (67, 48, 3),
        (69, 53, 89), (70, 100, 75), (71, 116, 71), (72, 80, 13), (73, 74, 70), (74, 70, 74), (75, 91, 11), (77, 65, 29),
        (78, 77, 74), (79, 75, 63), (80, 87, 93), (81, 82, 95), (82, 81, 87), (83, 99, 19), (84, 69, 74), (85, 88, 85),
        (86, 93, 53), (87, 89, 87), (88, 90, 88), (89, 23, 121), (90, 83, 5), (91, 25, 27), (93, 35, 45), (94, 78, 62),
        (95, 94, 69), (96, 97, 6), (97, 96, 111), (98, 114, 41), (99, 32, 35), (100, 84, 36), (101, 117, 92), (102, 86, 108),
        (104, 105, 111), (105, 73, 105), (106, 107, 106), (107, 123, 43), (108, 101, 108), (109, 27, 61), (110, 104, 110), (111, 110, 109),
        (113, 112, 7), (114, 113, 121), (115, 66, 39), (116, 3, 52), (118, 103, 125), (119, 118, 126), (120, 121, 120), (123, 115, 59),
        (124, 108, 60), (126, 29, 125),
    ],
    [
        (0, 1, 9), (2, 3, 11), (3, 11, 60), (4, 5, 13), (5, 21, 94), (6, 7, 15), (7, 23, 120), (9, 8, 1),
        (11, 10, 3), (13, 12, 13), (15, 14, 15), (17, 16, 18), (18, 2, 43), (19, 18, 20), (20, 27, 29), (22, 54, 22),
        (23, 22, 24), (24, 25, 18), (25, 24, 25), (27, 43, 91), (28, 20, 77), (29, 45, 95), (30, 6, 111), (31, 29, 31),
        (32, 33, 43), (33, 34, 36), (35, 50, 37), (36, 37, 47), (37, 38, 40), (38, 39, 41), (41, 42, 36), (42, 40, 42),
        (43, 58, 46), (44, 28, 78), (45, 32, 2), (46, 65, 30), (47, 46, 18), (48, 49, 52), (49, 48, 60), (50, 51, 54),
        (51, 55, 51), (52, 53, 56), (53, 99, 57), (54, 35, 54), (56, 57, 60), (57, 56, 52), (58, 59, 54), (59, 52, 63),
        (60, 61, 3), (61, 60, 56), (62, 63, 35), (63, 62, 58), (64, 76, 4), (65, 64, 77), (66, 67, 71), (67, 74, 79),
        (68, 69, 20), (69, 68, 73), (70, 71, 75), (71, 4, 68), (72, 79, 68), (73, 72, 77), (74, 75, 71), (76, 77, 73),
        (77, 73, 29), (78, 66, 46), (79, 78, 75), (80, 104, 14), (81, 80, 86), (82, 83, 88), (83, 84, 21), (84, 85, 37),
        (85, 19, 53), (86, 70, 54), (87, 103, 87), (88, 89, 86), (89, 92, 89), (90, 91, 5), (91, 41, 27), (92, 93, 90),
        (94, 110, 94), (95, 94, 92), (96, 97, 103), (97, 113, 1), (98, 82, 40), (99, 98, 105), (100, 101, 107), (101, 100, 54),
        (102, 36, 70), (103, 102, 86), (104, 88, 104), (106, 107, 105), (107, 106, 22), (109, 108, 107), (110, 44, 108), (111, 96, 110),
        (113, 112, 120), (114, 115, 122), (115, 114, 39), (117, 116, 124), (118, 87, 125), (119, 118, 103), (124, 125, 71), (126, 127, 126),
    ],
]
NRELAY = 4
NBUF = 1 + len(FIRST) + len(SECOND)


def holders():
    held = [{d: 0} for d in range(ND)]
    for n, edges in enumerate(FIRST):
        for _, there, tile in edges:
            held[there].setdefault(tile, 1 + n)
    source = np.zeros((len(SECOND), ND), np.int32)
    for n, edges in enumerate(SECOND):
        for here, _, tile in edges:
            source[n, here] = held[here][tile]
    for n, edges in enumerate(SECOND):
        for _, there, tile in edges:
            held[there].setdefault(tile, 1 + len(FIRST) + n)
    place = np.zeros((ND, 8), np.int32)
    for a in range(NR):
        for b in range(NC):
            for s in range(2):
                k = (a + b + s) % NR
                low = b < NR
                need = [
                    (k, b) if not low or k <= b else (b, k),
                    (b, k + NR) if low else (k, b) if k + NR <= b else (b - NR, k + NR),
                    (a, k) if a <= k else (k, a),
                    (a, k + NR),
                ]
                d = a * NC + b
                for kind, (r, c) in enumerate(need):
                    place[d, 4 * s + kind] = held[d][r * NC + c]
    return source, place


def slot_table(occupancy):
    i = np.arange(NB)
    before_col = (i[:, None] // CB == i[None, :] // CB) & (i[:, None] < i[None, :])
    panel = i[:, None] // CB == i[None, :] // CB
    before_row = (i[:, None] // CB % NR == i[None, :] // CB % NR) & (i[None, :] < i[:, None])
    occ = occupancy.astype(jnp.float32)
    dot = functools.partial(jnp.dot, precision=lax.Precision.HIGHEST)
    rank = dot(occ, jnp.asarray(before_col, jnp.float32)) + dot(
        jnp.asarray(before_row, jnp.float32), dot(occ, jnp.asarray(panel, jnp.float32))
    )
    return jnp.where(occupancy == 1, rank.astype(jnp.int32), -1)


def pick_kernel(source, lists, *refs):
    bufs, outs, sems = refs[: 1 + NRELAY], refs[1 + NRELAY : -1], refs[-1]
    here = lax.axis_index("row") * NC + lax.axis_index("col")
    for n, out in enumerate(outs):
        which = source[n * ND + here]
        for i in range(1 + NRELAY):

            @pl.when(which == i)
            def _():
                pltpu.make_async_copy(bufs[i], out, sems.at[n]).start()

    for n, out in enumerate(outs):
        pltpu.make_async_copy(bufs[0], out, sems.at[n]).wait()


def index_kernel(table, place, lists, blank, used):
    a = lax.axis_index("row")
    b = lax.axis_index("col")
    here = a * NC + b
    blank[...] = jnp.zeros_like(blank)

    def clear_used(t, carry):
        used[t] = 0
        return carry

    lax.fori_loop(0, 80, clear_used, 0)

    def step(t, n):
        s = t // 32
        kk = lax.rem(t // 2, 16)
        i = lax.rem(t, 2)
        half = kk // CB
        k = lax.rem(a + b + s, NR)
        inner = (half * NR + k) * CB + lax.rem(kk, CB)
        row = a * CB + i
        lslot = table[jnp.minimum(row, inner), jnp.maximum(row, inner)]
        lplace = (4 * s + 2 + half) * SLOTS + lslot
        turned = jnp.where(row > inner, 1, 0)

        def one_col(j, n0):
            n, fresh = n0
            col = b * CB + j
            rslot = table[jnp.minimum(inner, col), jnp.maximum(inner, col)]
            rplace = (4 * s + half) * SLOTS + rslot
            hit = rslot >= 0

            @pl.when(hit)
            def _():
                first = jnp.where(used[64 + i * CB + j] == 0, 1, 0)
                lists[n] = (
                    lplace
                    + (rplace << 6)
                    + ((i * CB + j) << 12)
                    + (turned << 16)
                    + (jnp.where(inner > col, 1, 0) << 17)
                    + (fresh << 18)
                    + (first << 19)
                    + ((1 - used[lplace]) << 21)
                    + ((1 - used[rplace]) << 22)
                )
                used[64 + i * CB + j] = 1
                used[lplace] = 1
                used[rplace] = 1

            one = jnp.where(hit, 1, 0)
            return n + one, fresh * (1 - one)

        return lax.cond(lslot >= 0, lambda m: lax.fori_loop(0, CB, one_col, (m, 1))[0], lambda m: m, n)

    count = lax.fori_loop(0, 64, step, 1)
    lists[0] = count

    def mark_last(q, carry):
        at = count - 1 - q
        code = lists[at]
        to = 64 + ((code >> 12) & 15)

        @pl.when(used[to] == 1)
        def _():
            lists[at] = code + (1 << 20)
            used[to] = 2

        return carry

    lax.fori_loop(0, count - 1, mark_last, 0)
    for t in range(16):
        lists[FETCH + 112 + t] = jnp.minimum(used[64 + t], 1)

    def by_buffer(buf, n):
        lists[FETCH + buf] = n

        def by_kind(kind, n):
            def by_slot(slot, n):
                @pl.when(used[kind * SLOTS + slot] == 1)
                def _():
                    lists[FETCH + n] = kind * SLOTS + slot

                return n + used[kind * SLOTS + slot]

            return lax.cond(
                place[here * 8 + kind] == buf, lambda m: lax.fori_loop(0, SLOTS, by_slot, m), lambda m: m, n
            )

        return lax.fori_loop(0, 8, by_kind, n)

    lists[FETCH + NBUF] = lax.fori_loop(0, NBUF, by_buffer, 32)


def product_kernel(lists, *refs):
    bufs = refs[:NBUF]
    blank, out, tiles, left, acc, sems, out_sems = refs[NBUF:]
    for n, buf in enumerate(bufs):

        def start(q, carry):
            t = lists[FETCH + q]
            pltpu.make_async_copy(buf.at[lax.rem(t, SLOTS)], tiles.at[t], sems.at[t]).start()
            return carry

        lax.fori_loop(lists[FETCH + n], lists[FETCH + n + 1], start, 0)

    def arrived(t):
        pltpu.make_async_copy(bufs[0].at[0], tiles.at[t], sems.at[t]).wait()

    def copy_out(t):
        return pltpu.make_async_copy(
            acc.at[t],
            out.at[pl.ds(pl.multiple_of(t // CB * BS, BS), BS), pl.ds(pl.multiple_of(lax.rem(t, CB) * BS, BS), BS)],
            out_sems.at[t],
        )

    def product(q, carry):
        code = lists[q]
        lt = tiles.at[code & 63]
        rt = tiles.at[(code >> 6) & 63]
        to = acc.at[(code >> 12) & 15]

        @pl.when(((code >> 21) & 1) == 1)
        def _():
            arrived(code & 63)

        @pl.when(((code >> 22) & 1) == 1)
        def _():
            arrived((code >> 6) & 63)

        @pl.when(((code >> 18) & 1) == 1)
        def _():
            @pl.when(((code >> 16) & 1) == 0)
            def _():
                left[...] = lt[...]

            @pl.when(((code >> 16) & 1) == 1)
            def _():
                left[...] = lt[...].T

        @pl.when(((code >> 19) & 1) == 1)
        def _():
            to[...] = jnp.zeros_like(to)

        @pl.when(((code >> 17) & 1) == 0)
        def _():
            to[...] += jnp.dot(left[...], rt[...], preferred_element_type=jnp.float32)

        @pl.when(((code >> 17) & 1) == 1)
        def _():
            to[...] += lax.dot_general(
                left[...], rt[...], (((1,), (1,)), ((), ())), preferred_element_type=jnp.float32
            )

        @pl.when(((code >> 20) & 1) == 1)
        def _():
            copy_out((code >> 12) & 15).start()

        return carry

    lax.fori_loop(1, lists[0], product, 0)
    for t in range(16):

        @pl.when(lists[FETCH + 112 + t] == 1)
        def _():
            copy_out(t).wait()


def tile_shape():
    return jax.ShapeDtypeStruct((SLOTS, BS, BS), jnp.bfloat16)


SMEM = pl.BlockSpec(memory_space=pltpu.SMEM)
ANY = pl.BlockSpec(memory_space=pl.ANY)


def local(occupancy, stored):
    own = stored.reshape(SLOTS, BS, BS)
    source, place = holders()
    bufs = [own]
    for edges in FIRST:
        bufs.append(lax.ppermute(own, ("row", "col"), [(u, v) for u, v, _ in edges]))
    lists, blank = pl.pallas_call(
        index_kernel,
        out_shape=(
            jax.ShapeDtypeStruct((FETCH + 128,), jnp.int32),
            jax.ShapeDtypeStruct((SR * BS, CB * BS), jnp.float32),
        ),
        in_specs=[SMEM, SMEM],
        out_specs=(SMEM, pl.BlockSpec(memory_space=pltpu.VMEM)),
        scratch_shapes=[pltpu.SMEM((80,), jnp.int32)],
        cost_estimate=pl.CostEstimate(flops=10**9, bytes_accessed=4 * MIB, transcendentals=0),
        name="index",
    )(slot_table(occupancy), jnp.asarray(place.reshape(-1)))
    flat_source = jnp.asarray(source.reshape(-1))
    sends = pl.pallas_call(
        pick_kernel,
        out_shape=[pltpu.VMEM((SLOTS, BS, BS), jnp.bfloat16)] * len(SECOND),
        in_specs=[SMEM, SMEM] + [ANY] * (1 + NRELAY),
        out_specs=[pl.BlockSpec(memory_space=pltpu.VMEM)] * len(SECOND),
        compiler_params=pltpu.CompilerParams(vmem_limit_bytes=16 * MIB),
        scratch_shapes=[pltpu.SemaphoreType.DMA((len(SECOND),))],
        cost_estimate=pl.CostEstimate(flops=0, bytes_accessed=2 * MIB, transcendentals=0),
        name="pick",
    )(flat_source, lists, *bufs[: 1 + NRELAY])
    later = [
        lax.ppermute(send, ("row", "col"), [(u, v) for u, v, _ in edges])
        for send, edges in zip(sends, SECOND, strict=True)
    ]
    bufs += later
    return pl.pallas_call(
        product_kernel,
        out_shape=jax.ShapeDtypeStruct((SR * BS, CB * BS), jnp.float32),
        in_specs=[SMEM] + [ANY] * (NBUF + 1),
        out_specs=ANY,
        scratch_shapes=[
            pltpu.VMEM((64, BS, BS), jnp.bfloat16),
            pltpu.VMEM((BS, BS), jnp.bfloat16),
            pltpu.VMEM((16, BS, BS), jnp.float32),
            pltpu.SemaphoreType.DMA((64,)),
            pltpu.SemaphoreType.DMA((16,)),
        ],
        input_output_aliases={1 + NBUF: 0},
        compiler_params=pltpu.CompilerParams(vmem_limit_bytes=60 * MIB),
        cost_estimate=pl.CostEstimate(flops=10**9, bytes_accessed=12 * MIB, transcendentals=0),
        name="products",
    )(lists, *bufs, blank)


def solution(mesh):
    placed = (P(), P("row", "col", None, None, None))
    return jax.shard_map(
        local, mesh=mesh, in_specs=placed, out_specs=P("row", "col"), check_vma=False
    )
```

```python
import functools

import jax
import jax.numpy as jnp
import numpy as np
from jax import lax
from jax.experimental import pallas as pl
from jax.experimental.pallas import tpu as pltpu
from jax.sharding import PartitionSpec as P

BS = 256
CB = 8
SLOTS = 8
SR = 2
NB = 128
NR = 8
NC = 16
ND = NR * NC
MIB = 1024 * 1024
FETCH = 640

FIRST = [
    [
        (1, 9, 1), (3, 2, 3), (5, 4, 5), (9, 8, 9), (11, 10, 11), (17, 29, 17), (18, 17, 18), (19, 18, 19),
        (20, 33, 20), (21, 20, 21), (22, 107, 22), (23, 81, 23), (25, 16, 25), (28, 27, 28), (29, 28, 29), (30, 21, 30),
        (31, 30, 31), (35, 99, 35), (36, 41, 36), (38, 35, 38), (39, 115, 39), (40, 37, 40), (43, 26, 43), (46, 43, 46),
        (52, 116, 52), (53, 57, 53), (54, 101, 54), (55, 52, 55), (56, 61, 56), (58, 63, 58), (60, 56, 60), (62, 50, 62),
        (68, 64, 68), (69, 117, 69), (70, 86, 70), (71, 66, 71), (73, 84, 73), (76, 124, 76), (77, 109, 77), (85, 80, 85),
        (86, 103, 86), (87, 82, 87), (94, 5, 94), (95, 90, 95), (102, 118, 102), (103, 22, 103), (104, 105, 104), (105, 89, 105),
        (106, 58, 106), (108, 102, 108), (110, 111, 110), (111, 108, 111), (119, 7, 119), (121, 122, 121), (124, 60, 124),
    ],
    [
        (0, 12, 0), (1, 16, 1), (2, 10, 2), (3, 60, 3), (4, 64, 4), (5, 53, 5), (6, 96, 6), (8, 7, 8),
        (10, 1, 10), (11, 75, 11), (12, 11, 12), (13, 45, 13), (14, 80, 14), (15, 124, 15), (17, 113, 17), (18, 47, 18),
        (19, 26, 19), (20, 27, 20), (21, 83, 21), (22, 28, 22), (23, 121, 23), (24, 23, 24), (27, 91, 27), (28, 19, 28),
        (29, 77, 29), (30, 46, 30), (31, 22, 31), (34, 114, 34), (35, 18, 35), (36, 100, 36), (37, 35, 37), (38, 43, 38),
        (39, 37, 39), (40, 24, 40), (41, 98, 41), (42, 39, 42), (43, 32, 43), (44, 108, 44), (45, 93, 45), (46, 44, 46),
        (47, 63, 47), (51, 3, 51), (52, 48, 52), (53, 86, 53), (54, 50, 54), (55, 71, 55), (56, 67, 56), (57, 61, 57),
        (58, 55, 58), (59, 56, 59), (60, 49, 60), (61, 57, 61), (63, 59, 63), (68, 72, 68), (69, 20, 69), (70, 73, 70),
        (71, 52, 71), (72, 76, 72), (73, 41, 73), (74, 84, 74), (75, 70, 75), (76, 8, 76), (77, 65, 77), (78, 66, 78),
        (79, 36, 79), (85, 117, 85), (86, 88, 86), (88, 82, 88), (89, 69, 89), (90, 42, 90), (91, 94, 91), (92, 95, 92),
        (93, 13, 93), (94, 81, 94), (95, 29, 95), (102, 106, 102), (103, 119, 103), (104, 38, 104), (105, 54, 105), (106, 74, 106),
        (107, 109, 107), (109, 111, 109), (110, 118, 110), (111, 97, 111), (119, 112, 119), (121, 105, 121), (122, 123, 122), (123, 115, 123),
        (124, 125, 124), (125, 126, 125), (127, 15, 127),
    ],
    [
        (1, 97, 1), (2, 45, 2), (3, 11, 3), (5, 90, 5), (6, 14, 6), (7, 23, 7), (9, 0, 9), (10, 27, 10),
        (11, 2, 11), (12, 76, 12), (13, 4, 13), (14, 30, 14), (15, 6, 15), (17, 16, 17), (18, 24, 18), (19, 83, 19),
        (20, 19, 20), (21, 49, 21), (22, 20, 22), (23, 22, 23), (25, 121, 25), (26, 9, 26), (27, 18, 27), (28, 94, 28),
        (29, 61, 29), (30, 29, 30), (34, 39, 34), (35, 54, 35), (36, 33, 36), (37, 43, 37), (38, 100, 38), (40, 98, 40),
        (41, 38, 41), (42, 32, 42), (43, 107, 43), (44, 41, 44), (45, 127, 45), (46, 78, 46), (47, 36, 47), (51, 48, 51),
        (52, 70, 52), (53, 85, 53), (54, 58, 54), (55, 116, 55), (56, 40, 56), (57, 53, 57), (58, 10, 58), (59, 123, 59),
        (60, 124, 60), (61, 50, 61), (62, 47, 62), (69, 65, 69), (70, 66, 70), (71, 74, 71), (72, 56, 72), (73, 69, 73),
        (74, 26, 74), (75, 79, 75), (77, 28, 77), (78, 44, 78), (79, 67, 79), (85, 5, 85), (86, 21, 86), (87, 117, 87),
        (88, 91, 88), (89, 73, 89), (90, 92, 90), (91, 101, 91), (93, 80, 93), (94, 126, 94), (95, 81, 95), (102, 103, 102),
        (103, 96, 103), (105, 99, 105), (107, 86, 107), (108, 109, 108), (111, 104, 111), (119, 120, 119), (120, 113, 120), (121, 89, 121),
        (122, 114, 122), (123, 75, 123), (124, 87, 124), (125, 118, 125), (126, 119, 126),
    ],
    [
        (0, 8, 0), (1, 63, 1), (2, 82, 2), (3, 67, 3), (4, 12, 4), (5, 37, 5), (6, 5, 6), (7, 113, 7),
        (8, 15, 8), (9, 105, 9), (10, 40, 10), (11, 56, 11), (12, 48, 12), (13, 72, 13), (14, 6, 14), (15, 120, 15),
        (17, 1, 17), (18, 38, 18), (19, 53, 19), (20, 68, 20), (21, 19, 21), (22, 65, 22), (23, 97, 23), (24, 31, 24),
        (26, 24, 26), (27, 26, 27), (28, 41, 28), (29, 20, 29), (30, 89, 30), (31, 47, 31), (34, 32, 34), (35, 62, 35),
        (36, 70, 36), (37, 84, 37), (38, 54, 38), (39, 36, 39), (41, 9, 41), (42, 10, 42), (43, 18, 43), (44, 33, 44),
        (45, 58, 45), (46, 35, 46), (47, 44, 47), (52, 57, 52), (53, 49, 53), (54, 86, 54), (55, 59, 55), (56, 52, 56),
        (57, 25, 57), (58, 115, 58), (59, 55, 59), (60, 3, 60), (61, 109, 61), (62, 94, 62), (63, 79, 63), (68, 71, 68),
        (69, 95, 69), (70, 102, 70), (71, 124, 71), (72, 75, 72), (73, 76, 73), (74, 78, 74), (75, 11, 75), (76, 64, 76),
        (77, 73, 77), (78, 74, 78), (79, 60, 79), (85, 87, 85), (86, 81, 86), (87, 90, 87), (88, 42, 88), (89, 83, 89),
        (90, 69, 90), (91, 27, 91), (92, 101, 92), (93, 88, 93), (94, 29, 94), (95, 21, 95), (102, 96, 102), (103, 104, 103),
        (104, 98, 104), (105, 106, 105), (106, 99, 106), (107, 100, 107), (108, 110, 108), (109, 13, 109), (110, 126, 110), (111, 30, 111),
        (120, 7, 120), (121, 114, 121), (123, 116, 123), (124, 117, 124), (126, 14, 126), (127, 112, 127),
    ],
]
SECOND = [
    [
        (0, 112, 0), (1, 16, 10), (2, 48, 11), (3, 32, 3), (4, 11, 4), (5, 13, 5), (6, 22, 6), (7, 15, 7),
        (8, 4, 76), (9, 24, 9), (10, 9, 10), (11, 116, 75), (12, 3, 12), (13, 29, 109), (14, 30, 126), (15, 0, 8),
        (16, 31, 25), (17, 1, 18), (18, 2, 35), (19, 27, 21), (20, 87, 69), (21, 5, 86), (22, 21, 31), (23, 39, 23),
        (24, 17, 26), (25, 23, 25), (26, 25, 19), (27, 77, 20), (28, 33, 28), (30, 46, 14), (31, 81, 31), (32, 41, 43),
        (33, 18, 36), (35, 50, 46), (36, 82, 47), (37, 44, 39), (38, 36, 38), (39, 122, 42), (40, 45, 40), (41, 26, 44),
        (42, 47, 42), (43, 92, 37), (44, 74, 47), (46, 62, 30), (47, 43, 62), (48, 115, 51), (49, 53, 21), (50, 35, 61),
        (53, 61, 19), (54, 38, 105), (55, 54, 58), (56, 52, 72), (57, 79, 52), (58, 42, 45), (59, 63, 59), (61, 49, 61),
        (62, 58, 62), (63, 51, 63), (64, 68, 4), (65, 98, 22), (66, 65, 70), (67, 83, 3), (68, 84, 20), (69, 72, 69),
        (70, 78, 36), (71, 123, 55), (72, 88, 13), (73, 57, 89), (74, 20, 78), (75, 71, 123), (76, 64, 12), (77, 19, 29),
        (78, 94, 78), (79, 67, 63), (80, 95, 85), (81, 89, 94), (82, 126, 87), (83, 91, 21), (84, 69, 37), (85, 101, 53),
        (86, 70, 107), (87, 37, 87), (88, 111, 86), (89, 73, 30), (90, 80, 5), (91, 107, 27), (92, 86, 92), (93, 34, 45),
        (94, 93, 91), (95, 12, 92), (96, 105, 6), (97, 114, 23), (98, 97, 104), (99, 40, 35), (100, 66, 38), (101, 109, 54),
        (102, 110, 70), (103, 118, 86), (104, 106, 104), (105, 121, 9), (106, 108, 106), (107, 59, 107), (109, 102, 109), (110, 28, 108),
        (111, 127, 111), (112, 120, 127), (113, 96, 7), (114, 55, 122), (115, 99, 58), (116, 100, 52), (117, 125, 87), (118, 6, 110),
        (119, 103, 126), (120, 104, 15), (121, 113, 25), (122, 90, 122), (123, 124, 123), (124, 117, 71), (126, 14, 110), (127, 119, 127),
    ],
    [
        (0, 7, 0), (1, 32, 10), (3, 27, 60), (4, 75, 4), (5, 64, 5), (6, 5, 14), (7, 120, 7), (8, 12, 76),
        (9, 25, 41), (10, 26, 58), (11, 56, 12), (12, 4, 12), (13, 61, 13), (15, 112, 8), (16, 1, 25), (17, 23, 17),
        (18, 33, 27), (19, 49, 28), (20, 86, 69), (21, 37, 95), (22, 6, 103), (23, 30, 23), (24, 106, 26), (25, 9, 25),
        (26, 16, 26), (27, 90, 10), (28, 29, 22), (29, 24, 17), (30, 88, 14), (31, 97, 24), (32, 114, 42), (33, 18, 44),
        (34, 2, 34), (35, 36, 46), (36, 52, 79), (37, 45, 39), (38, 22, 104), (39, 40, 34), (40, 46, 40), (41, 42, 44),
        (42, 84, 90), (43, 108, 38), (44, 66, 47), (45, 38, 2), (47, 105, 31), (48, 78, 52), (49, 35, 53), (50, 19, 61),
        (53, 62, 19), (54, 50, 38), (55, 3, 59), (56, 48, 59), (57, 58, 53), (58, 54, 106), (59, 60, 55), (60, 44, 79),
        (61, 57, 29), (63, 31, 1), (64, 71, 76), (65, 81, 22), (66, 65, 78), (67, 83, 56), (68, 76, 20), (69, 73, 69),
        (70, 69, 36), (71, 67, 55), (72, 68, 72), (73, 109, 70), (74, 70, 106), (76, 79, 76), (77, 125, 77), (78, 74, 46),
        (79, 95, 79), (80, 96, 14), (81, 113, 23), (82, 98, 2), (83, 17, 19), (84, 100, 74), (86, 94, 53), (87, 21, 87),
        (88, 72, 88), (89, 91, 89), (90, 89, 95), (91, 53, 88), (92, 28, 92), (93, 77, 45), (94, 92, 28), (95, 87, 92),
        (96, 80, 6), (99, 115, 35), (100, 99, 38), (101, 85, 91), (102, 101, 70), (103, 110, 86), (105, 39, 121), (106, 111, 102),
        (107, 43, 107), (108, 14, 111), (109, 93, 61), (111, 103, 109), (112, 127, 119), (113, 121, 7), (115, 82, 39), (116, 55, 123),
        (117, 118, 87), (118, 117, 125), (119, 126, 103), (120, 104, 120), (121, 122, 23), (123, 59, 123), (124, 116, 76), (126, 13, 94),
    ],
    [
        (1, 2, 10), (3, 53, 3), (4, 48, 4), (5, 12, 5), (6, 38, 6), (7, 14, 7), (8, 120, 8), (9, 1, 26),
        (10, 9, 2), (11, 27, 75), (12, 60, 12), (13, 5, 93), (14, 13, 14), (15, 7, 127), (16, 22, 1), (17, 114, 18),
        (18, 17, 27), (19, 18, 28), (20, 21, 22), (21, 28, 21), (22, 89, 31), (23, 29, 23), (24, 25, 26), (25, 83, 57),
        (26, 42, 74), (27, 26, 28), (28, 76, 28), (29, 31, 17), (30, 81, 30), (31, 113, 24), (32, 40, 43), (33, 34, 44),
        (35, 41, 35), (36, 90, 47), (37, 122, 39), (38, 46, 41), (39, 55, 39), (40, 106, 10), (41, 57, 73), (42, 58, 90),
        (43, 44, 38), (44, 110, 78), (45, 37, 2), (47, 97, 31), (48, 19, 52), (49, 69, 21), (50, 35, 62), (51, 63, 51),
        (52, 36, 71), (53, 54, 57), (54, 70, 38), (55, 51, 55), (56, 32, 11), (58, 100, 106), (59, 124, 55), (60, 52, 3),
        (61, 49, 29), (62, 59, 62), (63, 30, 1), (64, 3, 4), (67, 66, 79), (68, 116, 68), (69, 85, 90), (70, 77, 36),
        (71, 87, 71), (72, 64, 13), (73, 4, 77), (74, 73, 78), (75, 67, 72), (76, 72, 76), (78, 62, 46), (79, 75, 79),
        (80, 117, 93), (81, 80, 94), (82, 16, 2), (83, 65, 21), (84, 93, 37), (86, 20, 70), (87, 71, 124), (89, 84, 89),
        (90, 82, 5), (91, 86, 91), (93, 125, 93), (94, 88, 94), (95, 111, 95), (96, 98, 6), (97, 23, 1), (98, 47, 41),
        (99, 33, 35), (100, 107, 38), (101, 108, 54), (102, 104, 102), (104, 105, 103), (107, 99, 22), (108, 92, 44), (109, 43, 61),
        (110, 103, 110), (111, 118, 109), (114, 39, 122), (115, 123, 39), (116, 115, 55), (117, 101, 69), (118, 6, 102), (119, 127, 103),
        (120, 112, 15), (122, 74, 122), (124, 96, 15), (126, 45, 125), (127, 50, 45),
    ],
    [
        (0, 16, 9), (1, 0, 1), (2, 1, 2), (3, 19, 60), (4, 52, 4), (5, 106, 6), (7, 6, 7), (9, 122, 26),
        (10, 2, 42), (11, 72, 12), (12, 15, 0), (13, 95, 93), (14, 13, 6), (15, 31, 15), (17, 98, 18), (18, 33, 19),
        (19, 92, 21), (20, 4, 69), (21, 20, 30), (22, 38, 22), (23, 21, 23), (24, 8, 24), (25, 41, 57), (26, 10, 43),
        (27, 26, 20), (28, 12, 77), (29, 28, 30), (30, 22, 111), (31, 30, 24), (33, 49, 20), (34, 47, 34), (35, 34, 37),
        (38, 39, 18), (40, 24, 10), (41, 57, 28), (42, 37, 88), (43, 42, 37), (44, 36, 78), (45, 46, 2), (47, 45, 47),
        (48, 56, 51), (49, 50, 53), (50, 51, 62), (52, 71, 52), (53, 54, 19), (54, 55, 35), (56, 40, 11), (57, 58, 61),
        (58, 43, 45), (59, 11, 59), (60, 44, 124), (61, 62, 57), (63, 60, 63), (64, 67, 4), (65, 64, 69), (67, 48, 3),
        (69, 53, 89), (70, 100, 75), (71, 116, 71), (72, 80, 13), (73, 74, 70), (74, 70, 74), (75, 91, 11), (77, 65, 29),
        (78, 77, 74), (79, 75, 63), (80, 87, 93), (81, 82, 95), (82, 81, 87), (83, 99, 19), (84, 69, 74), (85, 88, 85),
        (86, 93, 53), (87, 89, 87), (88, 90, 88), (89, 23, 121), (90, 83, 5), (91, 25, 27), (93, 35, 45), (94, 78, 62),
        (95, 94, 69), (96, 97, 6), (97, 96, 111), (98, 114, 41), (99, 32, 35), (100, 84, 36), (101, 117, 92), (102, 86, 108),
        (104, 105, 111), (105, 73, 105), (106, 107, 106), (107, 123, 43), (108, 101, 108), (109, 27, 61), (110, 104, 110), (111, 110, 109),
        (113, 112, 7), (114, 113, 121), (115, 66, 39), (116, 3, 52), (118, 103, 125), (119, 118, 126), (120, 121, 120), (123, 115, 59),
        (124, 108, 60), (126, 29, 125),
    ],
    [
        (0, 1, 9), (2, 3, 11), (3, 11, 60), (4, 5, 13), (5, 21, 94), (6, 7, 15), (7, 23, 120), (9, 8, 1),
        (11, 10, 3), (13, 12, 13), (15, 14, 15), (17, 16, 18), (18, 2, 43), (19, 18, 20), (20, 27, 29), (22, 54, 22),
        (23, 22, 24), (24, 25, 18), (25, 24, 25), (27, 43, 91), (28, 20, 77), (29, 45, 95), (30, 6, 111), (31, 29, 31),
        (32, 33, 43), (33, 34, 36), (35, 50, 37), (36, 37, 47), (37, 38, 40), (38, 39, 41), (41, 42, 36), (42, 40, 42),
        (43, 58, 46), (44, 28, 78), (45, 32, 2), (46, 65, 30), (47, 46, 18), (48, 49, 52), (49, 48, 60), (50, 51, 54),
        (51, 55, 51), (52, 53, 56), (53, 99, 57), (54, 35, 54), (56, 57, 60), (57, 56, 52), (58, 59, 54), (59, 52, 63),
        (60, 61, 3), (61, 60, 56), (62, 63, 35), (63, 62, 58), (64, 76, 4), (65, 64, 77), (66, 67, 71), (67, 74, 79),
        (68, 69, 20), (69, 68, 73), (70, 71, 75), (71, 4, 68), (72, 79, 68), (73, 72, 77), (74, 75, 71), (76, 77, 73),
        (77, 73, 29), (78, 66, 46), (79, 78, 75), (80, 104, 14), (81, 80, 86), (82, 83, 88), (83, 84, 21), (84, 85, 37),
        (85, 19, 53), (86, 70, 54), (87, 103, 87), (88, 89, 86), (89, 92, 89), (90, 91, 5), (91, 41, 27), (92, 93, 90),
        (94, 110, 94), (95, 94, 92), (96, 97, 103), (97, 113, 1), (98, 82, 40), (99, 98, 105), (100, 101, 107), (101, 100, 54),
        (102, 36, 70), (103, 102, 86), (104, 88, 104), (106, 107, 105), (107, 106, 22), (109, 108, 107), (110, 44, 108), (111, 96, 110),
        (113, 112, 120), (114, 115, 122), (115, 114, 39), (117, 116, 124), (118, 87, 125), (119, 118, 103), (124, 125, 71), (126, 127, 126),
    ],
]
NRELAY = 4
NBUF = 1 + len(FIRST) + len(SECOND)


def holders():
    held = [{d: 0} for d in range(ND)]
    for n, edges in enumerate(FIRST):
        for _, there, tile in edges:
            held[there].setdefault(tile, 1 + n)
    source = np.zeros((len(SECOND), ND), np.int32)
    for n, edges in enumerate(SECOND):
        for here, _, tile in edges:
            source[n, here] = held[here][tile]
    for n, edges in enumerate(SECOND):
        for _, there, tile in edges:
            held[there].setdefault(tile, 1 + len(FIRST) + n)
    place = np.zeros((ND, 8), np.int32)
    for a in range(NR):
        for b in range(NC):
            for s in range(2):
                k = (a + b + s) % NR
                low = b < NR
                need = [
                    (k, b) if not low or k <= b else (b, k),
                    (b, k + NR) if low else (k, b) if k + NR <= b else (b - NR, k + NR),
                    (a, k) if a <= k else (k, a),
                    (a, k + NR),
                ]
                d = a * NC + b
                for kind, (r, c) in enumerate(need):
                    place[d, 4 * s + kind] = held[d][r * NC + c]
    return source, place


def slot_table(occupancy):
    i = np.arange(NB)
    before_col = (i[:, None] // CB == i[None, :] // CB) & (i[:, None] < i[None, :])
    panel = i[:, None] // CB == i[None, :] // CB
    before_row = (i[:, None] // CB % NR == i[None, :] // CB % NR) & (i[None, :] < i[:, None])
    occ = occupancy.astype(jnp.float32)
    dot = functools.partial(jnp.dot, precision=lax.Precision.HIGHEST)
    rank = dot(occ, jnp.asarray(before_col, jnp.float32)) + dot(
        jnp.asarray(before_row, jnp.float32), dot(occ, jnp.asarray(panel, jnp.float32))
    )
    return jnp.where(occupancy == 1, rank.astype(jnp.int32), -1)


def pick_kernel(source, lists, *refs):
    bufs, outs, sems = refs[: 1 + NRELAY], refs[1 + NRELAY : -1], refs[-1]
    here = lax.axis_index("row") * NC + lax.axis_index("col")
    for n, out in enumerate(outs):
        which = source[n * ND + here]
        for i in range(1 + NRELAY):

            @pl.when(which == i)
            def _():
                pltpu.make_async_copy(bufs[i], out, sems.at[n]).start()

    for n, out in enumerate(outs):
        pltpu.make_async_copy(bufs[0], out, sems.at[n]).wait()


def index_kernel(table, place, lists, blank, used):
    a = lax.axis_index("row")
    b = lax.axis_index("col")
    here = a * NC + b
    blank[...] = jnp.zeros_like(blank)

    def clear_used(t, carry):
        used[t] = 0
        return carry

    lax.fori_loop(0, 80, clear_used, 0)

    def step(t, n):
        s = t // 32
        kk = lax.rem(t // 2, 16)
        i = lax.rem(t, 2)
        half = kk // CB
        k = lax.rem(a + b + s, NR)
        inner = (half * NR + k) * CB + lax.rem(kk, CB)
        row = a * CB + i
        lslot = table[jnp.minimum(row, inner), jnp.maximum(row, inner)]
        lplace = (4 * s + 2 + half) * SLOTS + lslot
        turned = jnp.where(row > inner, 1, 0)

        def one_col(j, n0):
            n, fresh = n0
            col = b * CB + j
            rslot = table[jnp.minimum(inner, col), jnp.maximum(inner, col)]
            rplace = (4 * s + half) * SLOTS + rslot
            hit = rslot >= 0

            @pl.when(hit)
            def _():
                first = jnp.where(used[64 + i * CB + j] == 0, 1, 0)
                lists[n] = (
                    lplace
                    + (rplace << 6)
                    + ((i * CB + j) << 12)
                    + (turned << 16)
                    + (jnp.where(inner > col, 1, 0) << 17)
                    + (fresh << 18)
                    + (first << 19)
                    + ((1 - used[lplace]) << 21)
                    + ((1 - used[rplace]) << 22)
                )
                used[64 + i * CB + j] = 1
                used[lplace] = 1
                used[rplace] = 1

            one = jnp.where(hit, 1, 0)
            return n + one, fresh * (1 - one)

        return lax.cond(lslot >= 0, lambda m: lax.fori_loop(0, CB, one_col, (m, 1))[0], lambda m: m, n)

    count = lax.fori_loop(0, 64, step, 1)
    lists[0] = count

    def mark_last(q, carry):
        at = count - 1 - q
        code = lists[at]
        to = 64 + ((code >> 12) & 15)

        @pl.when(used[to] == 1)
        def _():
            lists[at] = code + (1 << 20)
            used[to] = 2

        return carry

    lax.fori_loop(0, count - 1, mark_last, 0)
    for t in range(16):
        lists[FETCH + 112 + t] = jnp.minimum(used[64 + t], 1)

    def by_buffer(buf, n):
        lists[FETCH + buf] = n

        def by_kind(kind, n):
            def by_slot(slot, n):
                @pl.when(used[kind * SLOTS + slot] == 1)
                def _():
                    lists[FETCH + n] = kind * SLOTS + slot

                return n + used[kind * SLOTS + slot]

            return lax.cond(
                place[here * 8 + kind] == buf, lambda m: lax.fori_loop(0, SLOTS, by_slot, m), lambda m: m, n
            )

        return lax.fori_loop(0, 8, by_kind, n)

    lists[FETCH + NBUF] = lax.fori_loop(0, NBUF, by_buffer, 32)


def product_kernel(lists, *refs):
    bufs = refs[:NBUF]
    blank, out, tiles, left, acc, sems, out_sems = refs[NBUF:]
    for n, buf in enumerate(bufs):

        def start(q, carry):
            t = lists[FETCH + q]
            pltpu.make_async_copy(buf.at[lax.rem(t, SLOTS)], tiles.at[t], sems.at[t]).start()
            return carry

        lax.fori_loop(lists[FETCH + n], lists[FETCH + n + 1], start, 0)

    def arrived(t):
        pltpu.make_async_copy(bufs[0].at[0], tiles.at[t], sems.at[t]).wait()

    def copy_out(t):
        return pltpu.make_async_copy(
            acc.at[t],
            out.at[pl.ds(pl.multiple_of(t // CB * BS, BS), BS), pl.ds(pl.multiple_of(lax.rem(t, CB) * BS, BS), BS)],
            out_sems.at[t],
        )

    def product(q, carry):
        code = lists[q]
        lt = tiles.at[code & 63]
        rt = tiles.at[(code >> 6) & 63]
        to = acc.at[(code >> 12) & 15]

        @pl.when(((code >> 21) & 1) == 1)
        def _():
            arrived(code & 63)

        @pl.when(((code >> 22) & 1) == 1)
        def _():
            arrived((code >> 6) & 63)

        @pl.when(((code >> 18) & 1) == 1)
        def _():
            @pl.when(((code >> 16) & 1) == 0)
            def _():
                left[...] = lt[...]

            @pl.when(((code >> 16) & 1) == 1)
            def _():
                left[...] = lt[...].T

        @pl.when(((code >> 19) & 1) == 1)
        def _():
            to[...] = jnp.zeros_like(to)

        @pl.when(((code >> 17) & 1) == 0)
        def _():
            to[...] += jnp.dot(left[...], rt[...], preferred_element_type=jnp.float32)

        @pl.when(((code >> 17) & 1) == 1)
        def _():
            to[...] += lax.dot_general(
                left[...], rt[...], (((1,), (1,)), ((), ())), preferred_element_type=jnp.float32
            )

        @pl.when(((code >> 20) & 1) == 1)
        def _():
            copy_out((code >> 12) & 15).start()

        return carry

    lax.fori_loop(1, lists[0], product, 0)
    for t in range(16):

        @pl.when(lists[FETCH + 112 + t] == 1)
        def _():
            copy_out(t).wait()


def tile_shape():
    return jax.ShapeDtypeStruct((SLOTS, BS, BS), jnp.bfloat16)


SMEM = pl.BlockSpec(memory_space=pltpu.SMEM)
ANY = pl.BlockSpec(memory_space=pl.ANY)


def local(occupancy, stored):
    own = stored.reshape(SLOTS, BS, BS)
    source, place = holders()
    bufs = [own]
    for edges in FIRST:
        bufs.append(lax.ppermute(own, ("row", "col"), [(u, v) for u, v, _ in edges]))
    lists, blank = pl.pallas_call(
        index_kernel,
        out_shape=(
            jax.ShapeDtypeStruct((FETCH + 128,), jnp.int32),
            jax.ShapeDtypeStruct((SR * BS, CB * BS), jnp.float32),
        ),
        in_specs=[SMEM, SMEM],
        out_specs=(SMEM, pl.BlockSpec(memory_space=pltpu.VMEM)),
        scratch_shapes=[pltpu.SMEM((80,), jnp.int32)],
        cost_estimate=pl.CostEstimate(flops=10**9, bytes_accessed=4 * MIB, transcendentals=0),
        name="index",
    )(slot_table(occupancy), jnp.asarray(place.reshape(-1)))
    flat_source = jnp.asarray(source.reshape(-1))
    sends = pl.pallas_call(
        pick_kernel,
        out_shape=[pltpu.VMEM((SLOTS, BS, BS), jnp.bfloat16)] * len(SECOND),
        in_specs=[SMEM, SMEM] + [ANY] * (1 + NRELAY),
        out_specs=[pl.BlockSpec(memory_space=pltpu.VMEM)] * len(SECOND),
        compiler_params=pltpu.CompilerParams(vmem_limit_bytes=16 * MIB),
        scratch_shapes=[pltpu.SemaphoreType.DMA((len(SECOND),))],
        cost_estimate=pl.CostEstimate(flops=0, bytes_accessed=2 * MIB, transcendentals=0),
        name="pick",
    )(flat_source, lists, *bufs[: 1 + NRELAY])
    later = [
        lax.ppermute(send, ("row", "col"), [(u, v) for u, v, _ in edges])
        for send, edges in zip(sends, SECOND, strict=True)
    ]
    bufs += later
    return pl.pallas_call(
        product_kernel,
        out_shape=jax.ShapeDtypeStruct((SR * BS, CB * BS), jnp.float32),
        in_specs=[SMEM] + [ANY] * (NBUF + 1),
        out_specs=ANY,
        scratch_shapes=[
            pltpu.VMEM((64, BS, BS), jnp.bfloat16),
            pltpu.VMEM((BS, BS), jnp.bfloat16),
            pltpu.VMEM((16, BS, BS), jnp.float32),
            pltpu.SemaphoreType.DMA((64,)),
            pltpu.SemaphoreType.DMA((16,)),
        ],
        input_output_aliases={1 + NBUF: 0},
        compiler_params=pltpu.CompilerParams(vmem_limit_bytes=20 * MIB),
        cost_estimate=pl.CostEstimate(flops=10**9, bytes_accessed=12 * MIB, transcendentals=0),
        name="products",
    )(lists, *bufs, blank)


def solution(mesh):
    placed = (P(), P("row", "col", None, None, None))
    return jax.shard_map(
        local, mesh=mesh, in_specs=placed, out_specs=P("row", "col"), check_vma=False
    )
```
